128 devices in a mesh: dp: 4 (over z), expert: 32 (over y, x, core).
Axes of the slice: x: 4, y: 4, z: 4, core: 2. Of those that a mesh axis runs over, the one named last changes fastest.
Arguments:
- grad_parts: bfloat16 [4, 8192, 7168], P('dp', 'expert'), may hold values from -3 to 3
- owner_slot: int32 [224], replicated, may hold values from 0 to 383, as said below
- stat_left: float32 [384, 512, 512], P(('dp', 'expert')), may hold values from -1 to 3, as said below
- stat_right: float32 [384, 512, 512], P(('dp', 'expert')), may hold values from -1 to 3, as said below
- root_left: bfloat16 [384, 512, 512], P(('dp', 'expert')), may hold values from -1 to 2, as said below
- root_right: bfloat16 [384, 512, 512], P(('dp', 'expert')), may hold values from -1 to 2, as said below
Outputs:
- new_left: float32 [384, 512, 512], P(('dp', 'expert'))
- new_right: float32 [384, 512, 512], P(('dp', 'expert'))
- updates: bfloat16 [8192, 7168], P('expert')
The draws below stay inside these ranges and needn't reach their ends.
Inputs may be any that keep to these rules, and one draw needn't show every extreme that they name: `owner_slot`: the entries are distinct; slot t lies on device t // 3 with devices counted dp first, then expert. No device holds more than 3 blocks and some device of every index along expert holds exactly 3. The devices of each index along expert hold 7 blocks together. Of the blocks that meet the rows of one device along expert, at most 1 lie on devices of one index along expert, and some index gets exactly 1. `stat_left`: each slot is symmetric with its diagonal in 0.3 to 3. `stat_right`: each slot is symmetric with its diagonal in 0.3 to 3. `root_left`: each slot is symmetric with its diagonal in 0.5 to 2. `root_right`: each slot is symmetric with its diagonal in 0.5 to 2.
All inputs are finite; a program needn't handle non-finite values.
Results may differ from the reference program's by a relative error of at most 0.017.
Values may be sent and summed in bfloat16 or wider, within the bound.
No kernel may reach another device: no remote copies, remote signals or barrier semaphores. Data moves between devices by JAX's collectives and lax.ppermute only.
A program may use at most 128 MiB of HBM per device.

```python
import math
import jax
import jax.numpy as jnp
from jax import lax

D = 7168
BLOCK = 512
ROWS = 8192
SHARD_ROWS = 256
WIDE_BLOCKS = 14
BLOCKS = 224
PIECES = 14
SLOTS = 3
ALL_SLOTS = 384
N_DP = 4
N_EXPERT = 32


def symmetric_draw(key, diag_low, diag_high, off_scale):
    diag_key, off_key = jax.random.split(key)
    diagonal = jnp.exp(jax.random.uniform(diag_key, (ALL_SLOTS, BLOCK), jnp.float32, math.log(diag_low), math.log(diag_high)))
    noise_part = jnp.clip(jax.random.normal(off_key, (ALL_SLOTS, BLOCK, BLOCK), jnp.float32), -4.0, 4.0)
    noise_part = noise_part * (off_scale / math.sqrt(BLOCK))
    mixed_part = (noise_part + jnp.swapaxes(noise_part, 1, 2)) * math.sqrt(0.5)
    identity = jnp.eye(BLOCK, dtype=jnp.float32)
    return mixed_part * (1.0 - identity) + diagonal[:, :, None] * identity


def draw_stat_left(key, part):
    key = jax.random.fold_in(key, 21)
    return symmetric_draw(key, 0.3, 3.0, 0.5)


def draw_stat_right(key, part):
    key = jax.random.fold_in(key, 22)
    return symmetric_draw(key, 0.3, 3.0, 0.5)


def draw_root_left(key, part):
    key = jax.random.fold_in(key, 23)
    return symmetric_draw(key, 0.5, 2.0, 0.5).astype(jnp.bfloat16)


def draw_root_right(key, part):
    key = jax.random.fold_in(key, 24)
    return symmetric_draw(key, 0.5, 2.0, 0.5).astype(jnp.bfloat16)


def draw_owner_slot(key, part):
    key = jax.random.fold_in(key, 11)
    blocks = jnp.arange(BLOCKS, dtype=jnp.int32)
    row_block = blocks // WIDE_BLOCKS
    block_group = row_block * BLOCK // max(SHARD_ROWS, BLOCK)
    within = blocks - block_group * PIECES
    group_count = BLOCKS // PIECES
    key_list = jax.random.split(jax.random.fold_in(key, 1), group_count)
    orders = jax.vmap(lambda subkey: jax.random.permutation(subkey, PIECES))(key_list).astype(jnp.int32)
    place_in = orders[block_group, within]
    column = (place_in + block_group * PIECES) % N_EXPERT
    relabel = jax.random.permutation(jax.random.fold_in(key, 2), N_EXPERT).astype(jnp.int32)
    column = relabel[column]
    same_col = column[None, :] == column[:, None]
    earlier = blocks[None, :] < blocks[:, None]
    col_rank = jnp.sum(same_col & earlier, axis=1).astype(jnp.int32)
    heavy_replica = jax.random.randint(jax.random.fold_in(key, 3), (N_EXPERT,), 0, N_DP).astype(jnp.int32)[column]
    rest_rank = jnp.maximum(col_rank - SLOTS, 0)
    replica = jnp.where(col_rank < SLOTS, heavy_replica, (heavy_replica + 1 + rest_rank % (N_DP - 1)) % N_DP)
    slot_pos = jnp.where(col_rank < SLOTS, col_rank, rest_rank // (N_DP - 1))
    return ((replica * N_EXPERT + column) * SLOTS + slot_pos).astype(jnp.int32)


def shard_levels(own_key, dims, cuts, smallest, top_value):
    factor_of = 1.0
    for axis_at, shards_of in cuts:
        heights = jax.random.uniform(jax.random.fold_in(jax.random.fold_in(own_key, 6), axis_at), (shards_of,), jnp.float32, smallest / len(cuts), top_value / len(cuts))
        factor_of = factor_of * jnp.repeat(jnp.exp(heights), dims[axis_at] // shards_of).reshape((-1,) + (1,) * (len(dims) - 1 - axis_at))
    return factor_of


def bell_draw(rng, dims, spread, most, shards=(), kind=jnp.bfloat16):
    array = jax.random.normal(rng, dims, jnp.float32) * spread
    if len(shards) > 0:
        array = shard_levels(rng, dims, shards, -0.22, 0.18) * array
    return jnp.clip(array, min=-most, max=most).astype(kind)


def setup_inputs(seed: int = 0) -> dict:
    splits = jax.random.split(jax.random.key(seed), 7)
    return {
        "grad_parts": bell_draw(splits[0], (N_DP, ROWS, D), 0.5, 3.0, ((0, 4), (1, 32))),
        "owner_slot": draw_owner_slot(jax.random.fold_in(splits[6], 71), 0),
        "stat_left": draw_stat_left(jax.random.fold_in(splits[6], 71), 0),
        "stat_right": draw_stat_right(jax.random.fold_in(splits[6], 71), 0),
        "root_left": draw_root_left(jax.random.fold_in(splits[6], 71), 0),
        "root_right": draw_root_right(jax.random.fold_in(splits[6], 71), 0),
    }


DECAY_RATE = 0.999


def per_block(items):
    block_low, left_root, right_root = items
    left_gram = jnp.dot(block_low, block_low.T, preferred_element_type=jnp.float32)
    right_gram = jnp.dot(block_low.T, block_low, preferred_element_type=jnp.float32)
    left_part = jnp.dot(left_root, block_low, preferred_element_type=jnp.float32).astype(jnp.bfloat16)
    update = jnp.dot(left_part, right_root, preferred_element_type=jnp.float32).astype(jnp.bfloat16)
    return left_gram, right_gram, update


def reference(grad_parts, owner_slot, stat_left, stat_right, root_left, root_right):
    summed = jnp.sum(grad_parts.astype(jnp.float32), axis=0).astype(jnp.bfloat16)
    summed = lax.optimization_barrier(summed)
    wide_count = D // BLOCK
    block_grid = summed.reshape(ROWS // BLOCK, BLOCK, wide_count, BLOCK).transpose(0, 2, 1, 3)
    block_grid = block_grid.reshape(BLOCKS, BLOCK, BLOCK)
    left_grams, right_grams, block_updates = lax.map(per_block, (block_grid, root_left[owner_slot], root_right[owner_slot]))
    new_left = (DECAY_RATE * stat_left).at[owner_slot].set(DECAY_RATE * stat_left[owner_slot] + (1.0 - DECAY_RATE) * left_grams)
    new_right = (DECAY_RATE * stat_right).at[owner_slot].set(DECAY_RATE * stat_right[owner_slot] + (1.0 - DECAY_RATE) * right_grams)
    updates = block_updates.reshape(ROWS // BLOCK, wide_count, BLOCK, BLOCK).transpose(0, 2, 1, 3).reshape(ROWS, D)
    return new_left, new_right, updates
```

```python
import jax
import jax.numpy as jnp
from jax import lax
from jax.sharding import PartitionSpec as P

DECAY_RATE = 0.999
CHUNKS = 2


def shards(grad_parts, owner_slot, stat_left, stat_right, root_left, root_right):
    dp_count = lax.axis_size("dp")
    expert_count = lax.axis_size("expert")
    shard_rows = grad_parts.shape[1]
    row_width = grad_parts.shape[2]
    slot_count, block_rows, block_cols = stat_left.shape
    wide_count = row_width // block_cols
    halves = block_rows // shard_rows
    row_blocks = expert_count // halves
    block_count = owner_slot.shape[0]
    chunk_rows = shard_rows // CHUNKS
    part_rows = chunk_rows // dp_count
    held_count = dp_count * slot_count

    my_expert = lax.axis_index("expert")
    blocks = jnp.arange(block_count, dtype=jnp.int32)
    column = owner_slot // slot_count % expert_count

    my_column = lax.dynamic_slice(column, (my_expert // halves * wide_count,), (wide_count,))
    to_column = my_column[None, :] == jnp.arange(expert_count, dtype=jnp.int32)[:, None]
    pieces = jnp.arange(wide_count, dtype=jnp.int32)
    send_piece = jnp.sum(jnp.where(to_column, pieces[None, :], 0), axis=1)

    held = jnp.arange(held_count, dtype=jnp.int32)
    slot_ids = (held // slot_count * expert_count + my_expert) * slot_count + held % slot_count
    holds = owner_slot[None, :] == slot_ids[:, None]
    held_row = jnp.sum(jnp.where(holds, blocks[None, :] // wide_count, 0), axis=1)
    held_used = jnp.any(holds, axis=1)
    row_ids = jnp.arange(row_blocks, dtype=jnp.int32)
    from_held = (held_row[None, :] == row_ids[:, None]) & held_used[None, :]
    back_held = jnp.sum(jnp.where(from_held, held[None, :], 0), axis=1)
    my_used = lax.dynamic_slice(held_used, (lax.axis_index("dp") * slot_count,), (slot_count,))

    gathered = []
    for chunk in range(CHUNKS):
        rows = grad_parts[0, chunk * chunk_rows : (chunk + 1) * chunk_rows]
        part = lax.psum_scatter(rows, "dp", scatter_dimension=0, tiled=True)
        layout = part.reshape(part_rows, wide_count, block_cols).transpose(1, 0, 2)
        incoming = lax.all_to_all(layout[send_piece], "expert", split_axis=0, concat_axis=0, tiled=True)
        by_row = incoming.reshape(row_blocks, halves, part_rows, block_cols)
        to_owner = by_row[held_row].reshape(dp_count, slot_count, halves, part_rows, block_cols)
        gathered.append(lax.all_to_all(to_owner, "dp", split_axis=0, concat_axis=0, tiled=True))
    grad = jnp.stack(gathered).transpose(2, 3, 0, 1, 4, 5)
    grad = grad.reshape(slot_count, block_rows, block_cols)
    grad = jnp.where(my_used[:, None, None], grad, jnp.zeros_like(grad))

    left_part = jnp.einsum("sij,sjk->sik", root_left, grad, preferred_element_type=jnp.float32).astype(jnp.bfloat16)
    update = jnp.einsum("sij,sjk->sik", left_part, root_right, preferred_element_type=jnp.float32).astype(jnp.bfloat16)
    update = update.reshape(slot_count, halves, CHUNKS, dp_count, part_rows, block_cols)

    out = []
    for chunk in range(CHUNKS):
        to_replica = update[:, :, chunk].transpose(2, 0, 1, 3, 4)
        column_part = lax.all_to_all(to_replica, "dp", split_axis=0, concat_axis=0, tiled=True)
        column_part = column_part.reshape(held_count, halves, part_rows, block_cols)
        to_rows = column_part[back_held].reshape(expert_count, part_rows, block_cols)
        returned = lax.all_to_all(to_rows, "expert", split_axis=0, concat_axis=0, tiled=True)
        part = returned[my_column].transpose(1, 0, 2).reshape(part_rows, row_width)
        out.append(lax.all_gather(part, "dp", axis=0, tiled=True))
    updates = jnp.concatenate(out, axis=0)

    left_gram = jnp.einsum("sij,skj->sik", grad, grad, preferred_element_type=jnp.float32)
    right_gram = jnp.einsum("sji,sjk->sik", grad, grad, preferred_element_type=jnp.float32)
    new_left = DECAY_RATE * stat_left + (1.0 - DECAY_RATE) * left_gram
    new_right = DECAY_RATE * stat_right + (1.0 - DECAY_RATE) * right_gram
    return new_left, new_right, updates


def solution(mesh):
    owned = P(("dp", "expert"), None, None)
    return jax.shard_map(
        shards,
        mesh=mesh,
        in_specs=(P("dp", "expert", None), P(), owned, owned, owned, owned),
        out_specs=(owned, owned, P("expert", None)),
        check_vma=False,
    )
```

```python
import functools

import jax
import jax.numpy as jnp
from jax import lax
from jax.experimental import pallas as pl
from jax.experimental.pallas import tpu as pltpu
from jax.sharding import PartitionSpec as P

DECAY_RATE = 0.999
CHUNKS = 2


def ring_shift(count, step):
    return [(i, (i + step) % count) for i in range(count)]


def ahead(x):
    return lax.ppermute(x, "dp", ring_shift(lax.axis_size("dp"), 1))


def behind(x):
    return lax.ppermute(x, "dp", ring_shift(lax.axis_size("dp"), -1))


def add(dtype, *terms):
    total = terms[0].astype(jnp.float32)
    for term in terms[1:]:
        total += term.astype(jnp.float32)
    return total.astype(dtype)


def sum_over_replicas(chunks):
    count = lax.axis_size("dp")
    me = lax.axis_index("dp")
    results = []
    after = None
    for rows in chunks:
        quarter = rows.shape[0] // count
        half = quarter // 2

        def part(offset, second):
            start = (me + offset) % count * quarter + second * half
            return lax.dynamic_slice_in_dim(rows, start, half, axis=0)

        outgoing = part(2, 0), part(2, 1), part(1, 0), part(3, 1)
        if after is not None:
            outgoing, after = lax.optimization_barrier((outgoing, after))
        relay_first = behind(outgoing[0])
        relay_second = ahead(outgoing[1])
        near_first = ahead(outgoing[2])
        near_second = behind(outgoing[3])
        after = add(rows.dtype, relay_first, part(3, 0)), add(rows.dtype, relay_second, part(1, 1))
        far_first = behind(after[0])
        far_second = ahead(after[1])
        first = add(rows.dtype, part(0, 0), near_first, far_first)
        second = add(rows.dtype, part(0, 1), near_second, far_second)
        results.append(jnp.concatenate([first, second], axis=0))
    return results


PLACES = ((0, 0), (0, 1), (1, 0), (1, 1), (2, 0), (2, 1), (3, 0), (3, 1))


def place_rows(base, me_ref, *refs):
    parts = refs[:7]
    out_ref, stage, in_sems, out_sems = refs[-4:]
    half = parts[-1].shape[0]
    me = me_ref[0]
    loads = []
    for i in range(7):
        first = 0 if i == 0 else i + 1
        width = 2 if i == 0 else 1
        loads.append(pltpu.make_async_copy(parts[i], stage.at[pl.ds(first * half, width * half)], in_sems.at[i]))
    for load in loads:
        load.start()
    stores = []
    for i, load in enumerate(loads):
        load.wait()
        first = 0 if i == 0 else i + 1
        width = 2 if i == 0 else 1
        offset, second = PLACES[first]
        start = pl.multiple_of(base + (me + offset) % 4 * 2 * half + second * half, half)
        store = pltpu.make_async_copy(
            stage.at[pl.ds(first * half, width * half)], out_ref.at[pl.ds(start, width * half)], out_sems.at[i]
        )
        store.start()
        stores.append(store)
    for store in stores:
        store.wait()


def gather_over_replicas(own, updates, base, total_rows):
    quarter, width = own.shape
    half = quarter // 2
    prev_first = ahead(own[:half])
    next_second = behind(own[half:])
    prev_second = ahead(own[half:])
    next_first = behind(own[:half])
    far_first = ahead(prev_first)
    far_second = behind(next_second)
    me = lax.axis_index("dp").astype(jnp.int32).reshape(1)
    any_spec = pl.BlockSpec(memory_space=pl.ANY)
    operands = [me, own, next_first, next_second, far_first, far_second, prev_first, prev_second]
    aliases = {}
    if updates is not None:
        aliases = {len(operands): 0}
        operands.append(updates)
    return pl.pallas_call(
        functools.partial(place_rows, base),
        out_shape=jax.ShapeDtypeStruct((total_rows, width), own.dtype),
        in_specs=[pl.BlockSpec(memory_space=pltpu.SMEM)] + [any_spec] * (len(operands) - 1),
        out_specs=any_spec,
        scratch_shapes=[
            pltpu.VMEM((8 * half, width), own.dtype),
            pltpu.SemaphoreType.DMA((7,)),
            pltpu.SemaphoreType.DMA((7,)),
        ],
        input_output_aliases=aliases,
        cost_estimate=pl.CostEstimate(flops=0, bytes_accessed=32 * half * width, transcendentals=0),
        name="place_rows",
    )(*operands)


def shards(grad_parts, owner_slot, stat_left, stat_right, root_left, root_right):
    dp_count = lax.axis_size("dp")
    expert_count = lax.axis_size("expert")
    shard_rows = grad_parts.shape[1]
    row_width = grad_parts.shape[2]
    slot_count, block_rows, block_cols = stat_left.shape
    wide_count = row_width // block_cols
    halves = block_rows // shard_rows
    row_blocks = expert_count // halves
    block_count = owner_slot.shape[0]
    chunk_rows = shard_rows // CHUNKS
    part_rows = chunk_rows // dp_count
    held_count = dp_count * slot_count

    my_expert = lax.axis_index("expert")
    blocks = jnp.arange(block_count, dtype=jnp.int32)
    column = owner_slot // slot_count % expert_count

    my_column = lax.dynamic_slice(column, (my_expert // halves * wide_count,), (wide_count,))
    to_column = my_column[None, :] == jnp.arange(expert_count, dtype=jnp.int32)[:, None]
    pieces = jnp.arange(wide_count, dtype=jnp.int32)
    send_piece = jnp.sum(jnp.where(to_column, pieces[None, :], 0), axis=1)

    held = jnp.arange(held_count, dtype=jnp.int32)
    slot_ids = (held // slot_count * expert_count + my_expert) * slot_count + held % slot_count
    holds = owner_slot[None, :] == slot_ids[:, None]
    held_row = jnp.sum(jnp.where(holds, blocks[None, :] // wide_count, 0), axis=1)
    held_used = jnp.any(holds, axis=1)
    row_ids = jnp.arange(row_blocks, dtype=jnp.int32)
    from_held = (held_row[None, :] == row_ids[:, None]) & held_used[None, :]
    back_held = jnp.sum(jnp.where(from_held, held[None, :], 0), axis=1)
    my_used = lax.dynamic_slice(held_used, (lax.axis_index("dp") * slot_count,), (slot_count,))

    chunks = [grad_parts[0, i * chunk_rows : (i + 1) * chunk_rows] for i in range(CHUNKS)]
    gathered = []
    for part in sum_over_replicas(chunks):
        layout = part.reshape(part_rows, wide_count, block_cols).transpose(1, 0, 2)
        incoming = lax.all_to_all(layout[send_piece], "expert", split_axis=0, concat_axis=0, tiled=True)
        by_row = incoming.reshape(row_blocks, halves, part_rows, block_cols)
        to_owner = by_row[held_row].reshape(dp_count, slot_count, halves, part_rows, block_cols)
        gathered.append(lax.all_to_all(to_owner, "dp", split_axis=0, concat_axis=0, tiled=True))
    grad = jnp.stack(gathered).transpose(2, 3, 0, 1, 4, 5)
    grad = grad.reshape(slot_count, block_rows, block_cols)
    grad = jnp.where(my_used[:, None, None], grad, jnp.zeros_like(grad))

    left_part = jnp.einsum("sij,sjk->sik", root_left, grad, preferred_element_type=jnp.float32).astype(jnp.bfloat16)
    update = jnp.einsum("sij,sjk->sik", left_part, root_right, preferred_element_type=jnp.float32).astype(jnp.bfloat16)
    update = update.reshape(slot_count, halves, CHUNKS, dp_count, part_rows, block_cols)

    updates = None
    for chunk in range(CHUNKS):
        to_replica = update[:, :, chunk].transpose(2, 0, 1, 3, 4)
        column_part = lax.all_to_all(to_replica, "dp", split_axis=0, concat_axis=0, tiled=True)
        column_part = column_part.reshape(held_count, halves, part_rows, block_cols)
        to_rows = column_part[back_held].reshape(expert_count, part_rows, block_cols)
        returned = lax.all_to_all(to_rows, "expert", split_axis=0, concat_axis=0, tiled=True)
        own = returned[my_column].transpose(1, 0, 2).reshape(part_rows, row_width)
        updates = gather_over_replicas(own, updates, chunk * chunk_rows, shard_rows)

    left_gram = jnp.einsum("sij,skj->sik", grad, grad, preferred_element_type=jnp.float32)
    right_gram = jnp.einsum("sji,sjk->sik", grad, grad, preferred_element_type=jnp.float32)
    new_left = DECAY_RATE * stat_left + (1.0 - DECAY_RATE) * left_gram
    new_right = DECAY_RATE * stat_right + (1.0 - DECAY_RATE) * right_gram
    return new_left, new_right, updates


def solution(mesh):
    owned = P(("dp", "expert"), None, None)
    return jax.shard_map(
        shards,
        mesh=mesh,
        in_specs=(P("dp", "expert", None), P(), owned, owned, owned, owned),
        out_specs=(owned, owned, P("expert", None)),
        check_vma=False,
    )
```

```python
import functools

import jax
import jax.numpy as jnp
from jax import lax
from jax.experimental import pallas as pl
from jax.experimental.pallas import tpu as pltpu
from jax.sharding import PartitionSpec as P

DECAY_RATE = 0.999
CHUNKS = 2
ANY = pl.BlockSpec(memory_space=pl.ANY)
SMEM = pl.BlockSpec(memory_space=pltpu.SMEM)


def shift(x, step):
    count = lax.axis_size("dp")
    return lax.ppermute(x, "dp", [(i, (i + step) % count) for i in range(count)])


def add(*terms):
    total = terms[0].astype(jnp.float32)
    for term in terms[1:]:
        total += term.astype(jnp.float32)
    return total.astype(terms[0].dtype)


def run_all(copies):
    for copy in copies:
        copy.start()
    for copy in copies:
        copy.wait()


def cost(moved, flops=0):
    return pl.CostEstimate(flops=flops, bytes_accessed=moved, transcendentals=0)


def pack_kernel(base, index_ref, me_ref, grad_ref, next_ref, prev_ref, out_ref, own, near, far, pieces, in_sems, out_sems):
    rows = own.shape[0]
    wide_count, _, block_cols = pieces.shape
    start = pl.multiple_of(base + me_ref[0] * rows, rows)
    run_all(
        [
            pltpu.make_async_copy(grad_ref.at[0, pl.ds(start, rows)], own, in_sems.at[0]),
            pltpu.make_async_copy(next_ref, near, in_sems.at[1]),
            pltpu.make_async_copy(prev_ref, far, in_sems.at[2]),
        ]
    )
    for w in range(wide_count):
        cols = slice(w * block_cols, (w + 1) * block_cols)
        pieces[w] = add(own[:, cols], near[:, cols], far[:, cols])
    run_all(
        [
            pltpu.make_async_copy(pieces.at[index_ref[c]], out_ref.at[c], out_sems.at[c])
            for c in range(out_ref.shape[0])
        ]
    )


def pack(base, index, me, grad_parts, from_next, from_prev, block_cols):
    rows, width = from_next.shape
    dtype = from_next.dtype
    dests = index.shape[0]
    return pl.pallas_call(
        functools.partial(pack_kernel, base),
        out_shape=jax.ShapeDtypeStruct((dests, rows, block_cols), dtype),
        in_specs=[SMEM, SMEM, ANY, ANY, ANY],
        out_specs=ANY,
        scratch_shapes=[pltpu.VMEM((rows, width), dtype)] * 3
        + [
            pltpu.VMEM((width // block_cols, rows, block_cols), dtype),
            pltpu.SemaphoreType.DMA((3,)),
            pltpu.SemaphoreType.DMA((dests,)),
        ],
        cost_estimate=cost(8 * rows * width + 2 * dests * rows * block_cols),
        name="pack",
    )(index, me, grad_parts, from_next, from_prev)


def pick_kernel(inputs, index_ref, *refs):
    sources, outs, stage, in_sems, out_sems = refs[:inputs], refs[inputs:-3], refs[-3], refs[-2], refs[-1]
    each = sources[0].shape[0]
    run_all(
        [
            pltpu.make_async_copy(source, stage.at[pl.ds(i * each, each)], in_sems.at[i])
            for i, source in enumerate(sources)
        ]
    )
    copies = []
    for out in outs:
        for i in range(out.shape[0]):
            at = len(copies)
            copies.append(pltpu.make_async_copy(stage.at[index_ref[at]], out.at[i], out_sems.at[at]))
    run_all(copies)


def pick(index, sources, out_counts):
    each, *entry = sources[0].shape
    dtype = sources[0].dtype
    total = each * len(sources)
    taken = sum(out_counts)
    size = 2 * entry[0] * entry[1] * entry[2]
    return pl.pallas_call(
        functools.partial(pick_kernel, len(sources)),
        out_shape=[jax.ShapeDtypeStruct((n, *entry), dtype) for n in out_counts],
        in_specs=[SMEM] + [ANY] * len(sources),
        out_specs=[ANY] * len(out_counts),
        scratch_shapes=[
            pltpu.VMEM((total, *entry), dtype),
            pltpu.SemaphoreType.DMA((len(sources),)),
            pltpu.SemaphoreType.DMA((taken,)),
        ],
        cost_estimate=cost((total + taken) * size),
        name="pick",
    )(index, *sources)


def precondition_kernel(
    used_ref, me_ref, own_ref, *refs
):
    rel = (own_ref,) + refs[:3]
    second_ref, left_ref, right_ref, grad_ref, first_out = refs[3:8]
    rel_out = refs[8:12]
    grad, left, right, update, in_sems, root_sems, grad_sems, out_sems = refs[12:]
    slots = left.shape[0]
    count = second_ref.shape[0]
    block = left.shape[1]
    me = me_ref[0]
    roots = [
        pltpu.make_async_copy(left_ref, left, root_sems.at[0]),
        pltpu.make_async_copy(right_ref, right, root_sems.at[1]),
    ]
    loads = [
        pltpu.make_async_copy(rel[d], grad.at[:, :, 0, (me + count - d) % count], in_sems.at[d]) for d in range(count)
    ] + [
        pltpu.make_async_copy(second_ref.at[q], grad.at[:, :, 1, q], in_sems.at[count + q]) for q in range(count)
    ]
    for copy in loads + roots:
        copy.start()
    for copy in loads + roots:
        copy.wait()
    outs = []
    for s in range(slots):
        whole = grad[s].reshape(block, block)
        whole = jnp.where(used_ref[s] > 0, whole, jnp.zeros_like(whole))
        grad[s] = whole.reshape(grad.shape[1:])
        keep = pltpu.make_async_copy(grad.at[s], grad_ref.at[s], grad_sems.at[s])
        keep.start()
        part = jnp.dot(left[s], whole, preferred_element_type=jnp.float32).astype(whole.dtype)
        result = jnp.dot(part, right[s], preferred_element_type=jnp.float32).astype(whole.dtype)
        update[s] = result.reshape(update.shape[1:])
        sends = [
            pltpu.make_async_copy(update.at[s, :, 0, q], first_out.at[q, s], out_sems.at[s, q]) for q in range(count)
        ] + [
            pltpu.make_async_copy(update.at[s, :, 1, (me + d) % count], rel_out[d].at[s], out_sems.at[s, count + d])
            for d in range(count)
        ]
        for copy in sends:
            copy.start()
        outs += sends + [keep]
    for copy in outs:
        copy.wait()


def precondition(used, me, rel, second, root_left, root_right):
    count = second.shape[0]
    slots, halves, rows, cols = rel[0].shape
    dtype = second.dtype
    block = root_left.shape[1]
    piece = jax.ShapeDtypeStruct(rel[0].shape, dtype)
    layout = (slots, halves, CHUNKS, count, rows, cols)
    outs = pl.pallas_call(
        precondition_kernel,
        out_shape=[jax.ShapeDtypeStruct(layout, dtype), jax.ShapeDtypeStruct(second.shape, dtype)] + [piece] * count,
        in_specs=[SMEM, SMEM] + [ANY] * (count + 3),
        out_specs=[ANY] * (count + 2),
        scratch_shapes=[
            pltpu.VMEM(layout, dtype),
            pltpu.VMEM(root_left.shape, dtype),
            pltpu.VMEM(root_right.shape, dtype),
            pltpu.VMEM(layout, dtype),
            pltpu.SemaphoreType.DMA((2 * count,)),
            pltpu.SemaphoreType.DMA((2,)),
            pltpu.SemaphoreType.DMA((slots,)),
            pltpu.SemaphoreType.DMA((slots, 2 * count)),
        ],
        compiler_params=pltpu.CompilerParams(vmem_limit_bytes=24 * 1024 * 1024),
        cost_estimate=cost(10 * slots * block * block, 4 * slots * block**3),
        name="precondition",
    )(used, me, *rel, second, root_left, root_right)
    return outs[0].reshape(slots, block, block), outs[1], outs[2:]


def unpack_kernel(index_ref, pieces_ref, out_ref, stage, in_sems, out_sem):
    cols = pieces_ref.shape[2]
    run_all(
        [
            pltpu.make_async_copy(pieces_ref.at[index_ref[w]], stage.at[:, pl.ds(w * cols, cols)], in_sems.at[w])
            for w in range(index_ref.shape[0])
        ]
    )
    run_all([pltpu.make_async_copy(stage, out_ref, out_sem)])


def unpack(index, pieces):
    _, rows, cols = pieces.shape
    shape = (rows, index.shape[0] * cols)
    return pl.pallas_call(
        unpack_kernel,
        out_shape=jax.ShapeDtypeStruct(shape, pieces.dtype),
        in_specs=[SMEM, ANY],
        out_specs=ANY,
        scratch_shapes=[
            pltpu.VMEM(shape, pieces.dtype),
            pltpu.SemaphoreType.DMA((index.shape[0],)),
            pltpu.SemaphoreType.DMA,
        ],
        cost_estimate=cost(4 * rows * shape[1]),
        name="unpack",
    )(index, pieces)


def place_kernel(base, me_ref, *refs):
    parts = refs[:5]
    out_ref, stage, in_sems, out_sems = refs[-4:]
    quarter = parts[0].shape[0]
    half = parts[3].shape[0]
    me = me_ref[0]
    places = ((0, 0), (1, 0), (3, 0), (2, 0), (2, half))
    loads, stores = [], []
    for i, (offset, down) in enumerate(places):
        rows = parts[i].shape[0]
        held = stage.at[pl.ds(offset * quarter + down, rows)]
        start = pl.multiple_of(base + (me + offset) % 4 * quarter + down, half)
        loads.append(pltpu.make_async_copy(parts[i], held, in_sems.at[i]))
        stores.append(pltpu.make_async_copy(held, out_ref.at[pl.ds(start, rows)], out_sems.at[i]))
    for load in loads:
        load.start()
    for load, store in zip(loads, stores):
        load.wait()
        store.start()
    for store in stores:
        store.wait()


def gather_over_replicas(me, own, updates, base, total_rows):
    quarter, width = own.shape
    half = quarter // 2
    from_prev = shift(own, 1)
    from_next = shift(own, -1)
    far_first = shift(from_prev[:half], 1)
    far_second = shift(from_next[half:], -1)
    operands = [me, own, from_next, from_prev, far_first, far_second]
    aliases = {}
    if updates is not None:
        aliases = {len(operands): 0}
        operands.append(updates)
    return pl.pallas_call(
        functools.partial(place_kernel, base),
        out_shape=jax.ShapeDtypeStruct((total_rows, width), own.dtype),
        in_specs=[SMEM] + [ANY] * (len(operands) - 1),
        out_specs=ANY,
        scratch_shapes=[
            pltpu.VMEM((4 * quarter, width), own.dtype),
            pltpu.SemaphoreType.DMA((5,)),
            pltpu.SemaphoreType.DMA((5,)),
        ],
        input_output_aliases=aliases,
        cost_estimate=cost(16 * quarter * width),
        name="place",
    )(*operands)


def expert_exchange(x):
    return lax.all_to_all(x, "expert", split_axis=0, concat_axis=0, tiled=True)


def replica_exchange(x):
    return lax.all_to_all(x, "dp", split_axis=0, concat_axis=0, tiled=True)


def shards(grad_parts, owner_slot, stat_left, stat_right, root_left, root_right):
    dp_count = lax.axis_size("dp")
    expert_count = lax.axis_size("expert")
    shard_rows = grad_parts.shape[1]
    row_width = grad_parts.shape[2]
    slot_count, block_rows, block_cols = stat_left.shape
    wide_count = row_width // block_cols
    halves = block_rows // shard_rows
    row_blocks = expert_count // halves
    block_count = owner_slot.shape[0]
    chunk_rows = shard_rows // CHUNKS
    quarter = chunk_rows // dp_count
    half = quarter // 2
    held_count = dp_count * slot_count

    my_expert = lax.axis_index("expert")
    my_dp = lax.axis_index("dp")
    me = my_dp.astype(jnp.int32).reshape(1)
    blocks = jnp.arange(block_count, dtype=jnp.int32)
    column = owner_slot // slot_count % expert_count

    my_column = lax.dynamic_slice(column, (my_expert // halves * wide_count,), (wide_count,))
    to_column = my_column[None, :] == jnp.arange(expert_count, dtype=jnp.int32)[:, None]
    pieces = jnp.arange(wide_count, dtype=jnp.int32)
    send_piece = jnp.sum(jnp.where(to_column, pieces[None, :], 0), axis=1)

    held = jnp.arange(held_count, dtype=jnp.int32)
    row_ids = jnp.arange(row_blocks, dtype=jnp.int32)

    def held_rows(replica):
        slot_ids = (replica * expert_count + my_expert) * slot_count + held % slot_count
        holds = owner_slot[None, :] == slot_ids[:, None]
        return jnp.sum(jnp.where(holds, blocks[None, :] // wide_count, 0), axis=1), jnp.any(holds, axis=1)

    def held_of_row(replica):
        rows, used = held_rows(replica)
        match = (rows[None, :] == row_ids[:, None]) & used[None, :]
        return jnp.sum(jnp.where(match, held[None, :], 0), axis=1)

    order = held // slot_count
    row_from, used = held_rows(order)
    row_from_rel, _ = held_rows((my_dp + order) % dp_count)
    back_from = held_of_row(order)
    back_from_rel = held_of_row((my_dp + dp_count - order) % dp_count)
    my_used = lax.dynamic_slice(used.astype(jnp.int32), (my_dp * slot_count,), (slot_count,))

    def part(chunk, offset, down, rows):
        start = chunk * chunk_rows + (my_dp + offset) % dp_count * quarter + down
        return lax.dynamic_slice(grad_parts, (0, start, 0), (1, rows, row_width))[0]

    def toward(chunk, from_next, from_prev):
        to_prev = add(part(chunk, 3, 0, quarter), jnp.pad(from_next, ((0, half), (0, 0))))
        to_next = add(part(chunk, 1, 0, quarter), jnp.pad(from_prev, ((half, 0), (0, 0))))
        return to_prev, to_next

    def relay(first, second):
        return shift(first, -1), shift(second, 1)

    def packed(chunk, to_prev, to_next):
        return pack(chunk * chunk_rows, send_piece, me, grad_parts, shift(to_prev, -1), shift(to_next, 1), block_cols)

    sends = toward(0, *relay(part(0, 2, 0, half), part(0, 2, half, half)))
    relays, sends = lax.optimization_barrier(((part(1, 2, 0, half), part(1, 2, half, half)), sends))
    first_packed = packed(0, *sends)
    sends = toward(1, *relay(*relays))
    sends, first_packed = lax.optimization_barrier((sends, first_packed))
    entry = (row_blocks, halves, quarter, block_cols)
    first_in = expert_exchange(first_packed).reshape(entry)
    second_packed = packed(1, *sends)
    rel = pick(row_from_rel, [first_in], (slot_count,) * dp_count)
    rel, second_packed = lax.optimization_barrier((rel, second_packed))
    rel = [rel[0]] + [shift(rel[d], d) for d in range(1, dp_count)]
    second_in = expert_exchange(second_packed).reshape(entry)
    (to_owner,) = pick(row_from, [second_in], (held_count,))
    second = replica_exchange(to_owner.reshape(dp_count, slot_count, *entry[1:]))

    grad, first_out, rel_out = precondition(my_used, me, rel, second, root_left, root_right)

    first_back = replica_exchange(first_out).reshape(held_count, *entry[1:])
    (to_rows,) = pick(back_from, [first_back], (row_blocks,))
    rel_out, to_rows = lax.optimization_barrier((rel_out, to_rows))
    rel_back = [rel_out[0]] + [shift(rel_out[d], d) for d in range(1, dp_count)]
    first_own = unpack(my_column, expert_exchange(to_rows.reshape(expert_count, quarter, block_cols)))
    (to_rows,) = pick(back_from_rel, rel_back, (row_blocks,))
    first_own, to_rows = lax.optimization_barrier((first_own, to_rows))
    second_own = unpack(my_column, expert_exchange(to_rows.reshape(expert_count, quarter, block_cols)))
    updates = gather_over_replicas(me, first_own, None, 0, shard_rows)
    updates = gather_over_replicas(me, second_own, updates, chunk_rows, shard_rows)

    left_gram = jnp.einsum("sij,skj->sik", grad, grad, preferred_element_type=jnp.float32)
    right_gram = jnp.einsum("sji,sjk->sik", grad, grad, preferred_element_type=jnp.float32)
    new_left = DECAY_RATE * stat_left + (1.0 - DECAY_RATE) * left_gram
    new_right = DECAY_RATE * stat_right + (1.0 - DECAY_RATE) * right_gram
    return new_left, new_right, updates


def solution(mesh):
    owned = P(("dp", "expert"), None, None)
    return jax.shard_map(
        shards,
        mesh=mesh,
        in_specs=(P("dp", "expert", None), P(), owned, owned, owned, owned),
        out_specs=(owned, owned, P("expert", None)),
        check_vma=False,
    )
```

```python
import functools

import jax
import jax.numpy as jnp
from jax import lax
from jax.experimental import pallas as pl
from jax.experimental.pallas import tpu as pltpu
from jax.sharding import PartitionSpec as P

DECAY_RATE = 0.999
CHUNKS = 2
ANY = pl.BlockSpec(memory_space=pl.ANY)
SMEM = pl.BlockSpec(memory_space=pltpu.SMEM)


def shift(x, step):
    count = lax.axis_size("dp")
    return lax.ppermute(x, "dp", [(i, (i + step) % count) for i in range(count)])


def add(*terms):
    total = terms[0].astype(jnp.float32)
    for term in terms[1:]:
        total += term.astype(jnp.float32)
    return total.astype(terms[0].dtype)


def run_all(copies):
    for copy in copies:
        copy.start()
    for copy in copies:
        copy.wait()


def cost(moved, flops=0):
    return pl.CostEstimate(flops=flops, bytes_accessed=moved, transcendentals=0)


def vmem(mebibytes):
    return pltpu.CompilerParams(vmem_limit_bytes=mebibytes * 1024 * 1024)


def pack_kernel(base, index_ref, me_ref, grad_ref, next_ref, prev_ref, out_ref, own, near, far, pieces, in_sems, out_sems):
    rows = own.shape[0]
    wide_count, _, block_cols = pieces.shape
    start = pl.multiple_of(base + me_ref[0] * rows, rows)
    run_all(
        [
            pltpu.make_async_copy(grad_ref.at[0, pl.ds(start, rows)], own, in_sems.at[0]),
            pltpu.make_async_copy(next_ref, near, in_sems.at[1]),
            pltpu.make_async_copy(prev_ref, far, in_sems.at[2]),
        ]
    )
    for w in range(wide_count):
        cols = slice(w * block_cols, (w + 1) * block_cols)
        pieces[w] = add(own[:, cols], near[:, cols], far[:, cols])
    run_all(
        [
            pltpu.make_async_copy(pieces.at[index_ref[c]], out_ref.at[c], out_sems.at[c])
            for c in range(out_ref.shape[0])
        ]
    )


def pack(base, index, me, grad_parts, from_next, from_prev, block_cols):
    rows, width = from_next.shape
    dtype = from_next.dtype
    dests = index.shape[0]
    return pl.pallas_call(
        functools.partial(pack_kernel, base),
        out_shape=jax.ShapeDtypeStruct((dests, rows, block_cols), dtype),
        in_specs=[SMEM, SMEM, ANY, ANY, ANY],
        out_specs=ANY,
        scratch_shapes=[pltpu.VMEM((rows, width), dtype)] * 3
        + [
            pltpu.VMEM((width // block_cols, rows, block_cols), dtype),
            pltpu.SemaphoreType.DMA((3,)),
            pltpu.SemaphoreType.DMA((dests,)),
        ],
        cost_estimate=cost(8 * rows * width + 2 * dests * rows * block_cols),
        compiler_params=vmem(4),
        name="pack",
    )(index, me, grad_parts, from_next, from_prev)


def pick_kernel(inputs, index_ref, *refs):
    sources, outs, stage, in_sems, out_sems = refs[:inputs], refs[inputs:-3], refs[-3], refs[-2], refs[-1]
    each = sources[0].shape[0]
    run_all(
        [
            pltpu.make_async_copy(source, stage.at[pl.ds(i * each, each)], in_sems.at[i])
            for i, source in enumerate(sources)
        ]
    )
    copies = []
    for out in outs:
        for i in range(out.shape[0]):
            at = len(copies)
            copies.append(pltpu.make_async_copy(stage.at[index_ref[at]], out.at[i], out_sems.at[at]))
    run_all(copies)


def pick(index, sources, out_counts):
    each, *entry = sources[0].shape
    dtype = sources[0].dtype
    total = each * len(sources)
    taken = sum(out_counts)
    size = 2 * entry[0] * entry[1] * entry[2]
    return pl.pallas_call(
        functools.partial(pick_kernel, len(sources)),
        out_shape=[jax.ShapeDtypeStruct((n, *entry), dtype) for n in out_counts],
        in_specs=[SMEM] + [ANY] * len(sources),
        out_specs=[ANY] * len(out_counts),
        scratch_shapes=[
            pltpu.VMEM((total, *entry), dtype),
            pltpu.SemaphoreType.DMA((len(sources),)),
            pltpu.SemaphoreType.DMA((taken,)),
        ],
        cost_estimate=cost((total + taken) * size),
        compiler_params=vmem(4),
        name="pick",
    )(index, *sources)


def precondition_kernel(chunk_pieces, used_ref, me_ref, *refs):
    pieces, (left_ref, right_ref, grad_ref) = refs[:chunk_pieces], refs[chunk_pieces : chunk_pieces + 3]
    outs = refs[chunk_pieces + 3 : 2 * chunk_pieces + 3]
    grad, left, right, update, in_sems, root_sems, grad_sems, out_sems = refs[2 * chunk_pieces + 3 :]
    slots, _, _, count = grad.shape[:4]
    block = left.shape[1]
    me = me_ref[0]
    loads = [
        pltpu.make_async_copy(piece, grad.at[:, :, i // count, (me + count - i % count) % count], in_sems.at[i])
        for i, piece in enumerate(pieces)
    ] + [
        pltpu.make_async_copy(left_ref, left, root_sems.at[0]),
        pltpu.make_async_copy(right_ref, right, root_sems.at[1]),
    ]
    run_all(loads)
    stores = []
    for s in range(slots):
        whole = grad[s].reshape(block, block)
        whole = jnp.where(used_ref[s] > 0, whole, jnp.zeros_like(whole))
        grad[s] = whole.reshape(grad.shape[1:])
        part = jnp.dot(left[s], whole, preferred_element_type=jnp.float32).astype(whole.dtype)
        result = jnp.dot(part, right[s], preferred_element_type=jnp.float32).astype(whole.dtype)
        update[s] = result.reshape(update.shape[1:])
        sends = [pltpu.make_async_copy(grad.at[s], grad_ref.at[s], grad_sems.at[s])] + [
            pltpu.make_async_copy(update.at[s, :, i // count, (me + i % count) % count], out.at[s], out_sems.at[s, i])
            for i, out in enumerate(outs)
        ]
        for copy in sends:
            copy.start()
        stores += sends
    for copy in stores:
        copy.wait()


def precondition(used, me, pieces, root_left, root_right):
    slots, halves, rows, cols = pieces[0].shape
    dtype = pieces[0].dtype
    block = root_left.shape[1]
    total = len(pieces)
    layout = (slots, halves, CHUNKS, total // CHUNKS, rows, cols)
    grad, *outs = pl.pallas_call(
        functools.partial(precondition_kernel, total),
        out_shape=[jax.ShapeDtypeStruct(layout, dtype)] + [jax.ShapeDtypeStruct(pieces[0].shape, dtype)] * total,
        in_specs=[SMEM, SMEM] + [ANY] * (total + 2),
        out_specs=[ANY] * (total + 1),
        scratch_shapes=[
            pltpu.VMEM(layout, dtype),
            pltpu.VMEM(root_left.shape, dtype),
            pltpu.VMEM(root_right.shape, dtype),
            pltpu.VMEM(layout, dtype),
            pltpu.SemaphoreType.DMA((total,)),
            pltpu.SemaphoreType.DMA((2,)),
            pltpu.SemaphoreType.DMA((slots,)),
            pltpu.SemaphoreType.DMA((slots, total)),
        ],
        compiler_params=vmem(16),
        cost_estimate=cost(10 * slots * block * block, 4 * slots * block**3),
        name="precondition",
    )(used, me, *pieces, root_left, root_right)
    return grad.reshape(slots, block, block), outs[: total // CHUNKS], outs[total // CHUNKS :]


def unpack_kernel(index_ref, pieces_ref, out_ref, stage, in_sems, out_sem):
    cols = pieces_ref.shape[2]
    run_all(
        [
            pltpu.make_async_copy(pieces_ref.at[index_ref[w]], stage.at[:, pl.ds(w * cols, cols)], in_sems.at[w])
            for w in range(index_ref.shape[0])
        ]
    )
    run_all([pltpu.make_async_copy(stage, out_ref, out_sem)])


def unpack(index, pieces):
    _, rows, cols = pieces.shape
    shape = (rows, index.shape[0] * cols)
    return pl.pallas_call(
        unpack_kernel,
        out_shape=jax.ShapeDtypeStruct(shape, pieces.dtype),
        in_specs=[SMEM, ANY],
        out_specs=ANY,
        scratch_shapes=[
            pltpu.VMEM(shape, pieces.dtype),
            pltpu.SemaphoreType.DMA((index.shape[0],)),
            pltpu.SemaphoreType.DMA,
        ],
        cost_estimate=cost(4 * rows * shape[1]),
        compiler_params=vmem(4),
        name="unpack",
    )(index, pieces)


def place_kernel(base, me_ref, *refs):
    parts = refs[:5]
    out_ref, stage, in_sems, out_sems = refs[-4:]
    quarter = parts[0].shape[0]
    half = parts[3].shape[0]
    me = me_ref[0]
    places = ((0, 0), (1, 0), (3, 0), (2, 0), (2, half))
    loads, stores = [], []
    for i, (offset, down) in enumerate(places):
        rows = parts[i].shape[0]
        held = stage.at[pl.ds(offset * quarter + down, rows)]
        start = pl.multiple_of(base + (me + offset) % 4 * quarter + down, half)
        loads.append(pltpu.make_async_copy(parts[i], held, in_sems.at[i]))
        stores.append(pltpu.make_async_copy(held, out_ref.at[pl.ds(start, rows)], out_sems.at[i]))
    for load in loads:
        load.start()
    for load, store in zip(loads, stores):
        load.wait()
        store.start()
    for store in stores:
        store.wait()


def spread(own):
    return shift(own, -1), shift(own, 1)


def spread_far(from_next, from_prev):
    half = from_prev.shape[0] // 2
    return shift(from_prev[:half], 1), shift(from_next[half:], -1)


def place(me, parts, updates, base, total_rows):
    quarter, width = parts[0].shape
    operands = [me, *parts]
    aliases = {}
    if updates is not None:
        aliases = {len(operands): 0}
        operands.append(updates)
    return pl.pallas_call(
        functools.partial(place_kernel, base),
        out_shape=jax.ShapeDtypeStruct((total_rows, width), parts[0].dtype),
        in_specs=[SMEM] + [ANY] * (len(operands) - 1),
        out_specs=ANY,
        scratch_shapes=[
            pltpu.VMEM((4 * quarter, width), parts[0].dtype),
            pltpu.SemaphoreType.DMA((5,)),
            pltpu.SemaphoreType.DMA((5,)),
        ],
        input_output_aliases=aliases,
        cost_estimate=cost(16 * quarter * width),
        compiler_params=vmem(4),
        name="place",
    )(*operands)


def expert_exchange(x):
    return lax.all_to_all(x, "expert", split_axis=0, concat_axis=0, tiled=True)


def replica_exchange(parts):
    return [parts[0]] + [shift(parts[d], d) for d in range(1, len(parts))]


def shards(grad_parts, owner_slot, stat_left, stat_right, root_left, root_right):
    dp_count = lax.axis_size("dp")
    expert_count = lax.axis_size("expert")
    shard_rows = grad_parts.shape[1]
    row_width = grad_parts.shape[2]
    slot_count, block_rows, block_cols = stat_left.shape
    wide_count = row_width // block_cols
    halves = block_rows // shard_rows
    row_blocks = expert_count // halves
    block_count = owner_slot.shape[0]
    chunk_rows = shard_rows // CHUNKS
    quarter = chunk_rows // dp_count
    half = quarter // 2
    held_count = dp_count * slot_count

    my_expert = lax.axis_index("expert")
    my_dp = lax.axis_index("dp")
    me = my_dp.astype(jnp.int32).reshape(1)
    blocks = jnp.arange(block_count, dtype=jnp.int32)
    column = owner_slot // slot_count % expert_count

    my_column = lax.dynamic_slice(column, (my_expert // halves * wide_count,), (wide_count,))
    to_column = my_column[None, :] == jnp.arange(expert_count, dtype=jnp.int32)[:, None]
    pieces = jnp.arange(wide_count, dtype=jnp.int32)
    send_piece = jnp.sum(jnp.where(to_column, pieces[None, :], 0), axis=1)

    held = jnp.arange(held_count, dtype=jnp.int32)
    row_ids = jnp.arange(row_blocks, dtype=jnp.int32)

    def held_rows(replica):
        slot_ids = (replica * expert_count + my_expert) * slot_count + held % slot_count
        holds = owner_slot[None, :] == slot_ids[:, None]
        return jnp.sum(jnp.where(holds, blocks[None, :] // wide_count, 0), axis=1), jnp.any(holds, axis=1)

    def held_of_row(replica):
        rows, used = held_rows(replica)
        match = (rows[None, :] == row_ids[:, None]) & used[None, :]
        return jnp.sum(jnp.where(match, held[None, :], 0), axis=1)

    ahead = held // slot_count
    row_from, used = held_rows((my_dp + ahead) % dp_count)
    back_from = held_of_row((my_dp + dp_count - ahead) % dp_count)
    my_used = used[:slot_count].astype(jnp.int32)

    def part(chunk, offset, down, rows):
        start = chunk * chunk_rows + (my_dp + offset) % dp_count * quarter + down
        return lax.dynamic_slice(grad_parts, (0, start, 0), (1, rows, row_width))[0]

    def toward(chunk, from_next, from_prev):
        to_prev = add(part(chunk, 3, 0, quarter), jnp.pad(from_next, ((0, half), (0, 0))))
        to_next = add(part(chunk, 1, 0, quarter), jnp.pad(from_prev, ((half, 0), (0, 0))))
        return to_prev, to_next

    def packed(chunk, to_prev, to_next):
        return pack(chunk * chunk_rows, send_piece, me, grad_parts, shift(to_prev, -1), shift(to_next, 1), block_cols)

    entry = (row_blocks, halves, quarter, block_cols)
    slots_of = (slot_count,) * dp_count

    def to_owners(incoming):
        return replica_exchange(pick(row_from, [incoming.reshape(entry)], slots_of))

    def to_rows(column_parts):
        (rows,) = pick(back_from, column_parts, (row_blocks,))
        return rows.reshape(expert_count, quarter, block_cols)

    from_next = shift(jnp.concatenate([part(chunk, 2, 0, half) for chunk in range(CHUNKS)]), -1)
    from_prev = shift(jnp.concatenate([part(chunk, 2, half, half) for chunk in range(CHUNKS)]), 1)
    first_packed = packed(0, *toward(0, from_next[:half], from_prev[:half]))
    sends = toward(1, from_next[half:], from_prev[half:])
    sends, first_packed = lax.optimization_barrier((sends, first_packed))
    first_in = expert_exchange(first_packed)
    second_in = expert_exchange(packed(1, *sends))
    first_owned = to_owners(first_in)
    first_owned, second_in = lax.optimization_barrier((first_owned, second_in))
    second_owned = to_owners(second_in)

    grad, first_out, second_out = precondition(my_used, me, first_owned + second_owned, root_left, root_right)

    first_back = replica_exchange(first_out)
    left_gram = jnp.einsum("sij,skj->sik", grad, grad, preferred_element_type=jnp.float32)
    right_gram = jnp.einsum("sji,sjk->sik", grad, grad, preferred_element_type=jnp.float32)
    new_left = DECAY_RATE * stat_left + (1.0 - DECAY_RATE) * left_gram
    new_right = DECAY_RATE * stat_right + (1.0 - DECAY_RATE) * right_gram
    first_back, new_left, new_right = lax.optimization_barrier((first_back, new_left, new_right))
    first_rows = to_rows(first_back)
    second_out, first_rows = lax.optimization_barrier((second_out, first_rows))
    first_in, second_back = lax.optimization_barrier((expert_exchange(first_rows), replica_exchange(second_out)))
    first_own = unpack(my_column, first_in)
    second_in = expert_exchange(to_rows(second_back))

    near = spread(first_own)
    far = spread_far(*near)
    far, second_in = lax.optimization_barrier((far, second_in))
    second_own = unpack(my_column, second_in)
    updates = place(me, (first_own, *near, *far), None, 0, shard_rows)
    near = spread(second_own)
    near, updates = lax.optimization_barrier((near, updates))
    updates = place(me, (second_own, *near, *spread_far(*near)), updates, chunk_rows, shard_rows)
    return new_left, new_right, updates


def solution(mesh):
    owned = P(("dp", "expert"), None, None)
    return jax.shard_map(
        shards,
        mesh=mesh,
        in_specs=(P("dp", "expert", None), P(), owned, owned, owned, owned),
        out_specs=(owned, owned, P("expert", None)),
        check_vma=False,
    )
```

```python
import functools

import jax
import jax.numpy as jnp
from jax import lax
from jax.experimental import pallas as pl
from jax.experimental.pallas import tpu as pltpu
from jax.sharding import PartitionSpec as P

DECAY_RATE = 0.999
CHUNKS = 2
ANY = pl.BlockSpec(memory_space=pl.ANY)
SMEM = pl.BlockSpec(memory_space=pltpu.SMEM)
HBM = pl.BlockSpec(memory_space=pltpu.HBM)


def shift(x, step):
    count = lax.axis_size("dp")
    return lax.ppermute(x, "dp", [(i, (i + step) % count) for i in range(count)])


def add(*terms):
    total = terms[0].astype(jnp.float32)
    for term in terms[1:]:
        total += term.astype(jnp.float32)
    return total.astype(terms[0].dtype)


def run_all(copies):
    for copy in copies:
        copy.start()
    for copy in copies:
        copy.wait()


def cost(moved, flops=0):
    return pl.CostEstimate(flops=flops, bytes_accessed=moved, transcendentals=0)


def vmem(mebibytes):
    return pltpu.CompilerParams(vmem_limit_bytes=mebibytes * 1024 * 1024)


def pack_kernel(index_ref, own_ref, next_ref, prev_ref, out_ref, own, near, far, pieces, in_sems, out_sems):
    wide_count, _, block_cols = pieces.shape
    run_all(
        [
            pltpu.make_async_copy(own_ref, own, in_sems.at[0]),
            pltpu.make_async_copy(next_ref, near, in_sems.at[1]),
            pltpu.make_async_copy(prev_ref, far, in_sems.at[2]),
        ]
    )
    for w in range(wide_count):
        cols = slice(w * block_cols, (w + 1) * block_cols)
        pieces[w] = add(own[:, cols], near[:, cols], far[:, cols])
    run_all(
        [
            pltpu.make_async_copy(pieces.at[index_ref[c]], out_ref.at[c], out_sems.at[c])
            for c in range(out_ref.shape[0])
        ]
    )


def pack(index, own, from_next, from_prev, block_cols):
    rows, width = own.shape
    dests = index.shape[0]
    return pl.pallas_call(
        pack_kernel,
        out_shape=jax.ShapeDtypeStruct((dests, rows, block_cols), own.dtype),
        in_specs=[SMEM, ANY, ANY, ANY],
        out_specs=ANY,
        scratch_shapes=[pltpu.VMEM((rows, width), own.dtype)] * 3
        + [
            pltpu.VMEM((width // block_cols, rows, block_cols), own.dtype),
            pltpu.SemaphoreType.DMA((3,)),
            pltpu.SemaphoreType.DMA((dests,)),
        ],
        cost_estimate=cost(8 * rows * width + 2 * dests * rows * block_cols),
        compiler_params=vmem(4),
        name="pack",
    )(index, own, from_next, from_prev)


def run_used(used_ref, copies):
    for start in (True, False):
        for i, copy in enumerate(copies):

            @pl.when(used_ref[i] > 0)
            def _():
                copy.start() if start else copy.wait()


def to_slots_kernel(row_ref, used_ref, rows_ref, *refs):
    outs, sems = refs[:-1], refs[-1]
    slots = outs[0].shape[0]
    run_used(
        used_ref,
        [
            pltpu.make_async_copy(rows_ref.at[row_ref[i]], outs[i // slots].at[i % slots], sems.at[i])
            for i in range(len(outs) * slots)
        ],
    )


def to_slots(row, used, rows, replicas):
    entry = rows.shape[1:]
    held = row.shape[0]
    return pl.pallas_call(
        to_slots_kernel,
        out_shape=[jax.ShapeDtypeStruct((held // replicas, *entry), rows.dtype)] * replicas,
        in_specs=[SMEM, SMEM, ANY],
        out_specs=[ANY] * replicas,
        scratch_shapes=[pltpu.SemaphoreType.DMA((held,))],
        cost_estimate=cost(4 * held * entry[0] * entry[1] * entry[2]),
        compiler_params=vmem(4),
        name="to_slots",
    )(row, used, rows)


def from_slots_kernel(row_ref, used_ref, *refs):
    parts, rows_ref, sems = refs[:-2], refs[-2], refs[-1]
    slots = parts[0].shape[0]
    run_used(
        used_ref,
        [
            pltpu.make_async_copy(parts[i // slots].at[i % slots], rows_ref.at[row_ref[i]], sems.at[i])
            for i in range(len(parts) * slots)
        ],
    )


def from_slots(row, used, parts, row_blocks):
    slots, *entry = parts[0].shape
    held = row.shape[0]
    return pl.pallas_call(
        from_slots_kernel,
        out_shape=jax.ShapeDtypeStruct((row_blocks, *entry), parts[0].dtype),
        in_specs=[SMEM, SMEM] + [ANY] * len(parts),
        out_specs=ANY,
        scratch_shapes=[pltpu.SemaphoreType.DMA((held,))],
        cost_estimate=cost(4 * held * entry[0] * entry[1] * entry[2]),
        compiler_params=vmem(4),
        name="from_slots",
    )(row, used, *parts)


def precondition_kernel(chunk_pieces, used_ref, me_ref, *refs):
    pieces, (left_ref, right_ref, grad_ref) = refs[:chunk_pieces], refs[chunk_pieces : chunk_pieces + 3]
    outs = refs[chunk_pieces + 3 : 2 * chunk_pieces + 3]
    grad, left, right, update, in_sems, root_sems, grad_sems, out_sems = refs[2 * chunk_pieces + 3 :]
    slots, _, _, count = grad.shape[:4]
    block = left.shape[1]
    me = me_ref[0]
    loads = [
        pltpu.make_async_copy(piece, grad.at[:, :, i // count, (me + count - i % count) % count], in_sems.at[i])
        for i, piece in enumerate(pieces)
    ]
    roots = [
        (
            pltpu.make_async_copy(left_ref.at[s], left.at[s], root_sems.at[0, s]),
            pltpu.make_async_copy(right_ref.at[s], right.at[s], root_sems.at[1, s]),
        )
        for s in range(slots)
    ]
    for pair in roots:
        for copy in pair:
            copy.start()
    run_all(loads)
    stores = []
    for s in range(slots):
        whole = grad[s].reshape(block, block)
        whole = jnp.where(used_ref[s] > 0, whole, jnp.zeros_like(whole))
        grad[s] = whole.reshape(grad.shape[1:])
        roots[s][0].wait()
        part = jnp.dot(left[s], whole, preferred_element_type=jnp.float32).astype(whole.dtype)
        roots[s][1].wait()
        result = jnp.dot(part, right[s], preferred_element_type=jnp.float32).astype(whole.dtype)
        update[s] = result.reshape(update.shape[1:])
        sends = [pltpu.make_async_copy(grad.at[s], grad_ref.at[s], grad_sems.at[s])] + [
            pltpu.make_async_copy(update.at[s, :, i // count, (me + i % count) % count], out.at[s], out_sems.at[s, i])
            for i, out in enumerate(outs)
        ]
        for copy in sends:
            copy.start()
        stores += sends
    for copy in stores:
        copy.wait()


def precondition(used, me, pieces, root_left, root_right):
    slots, halves, rows, cols = pieces[0].shape
    dtype = pieces[0].dtype
    block = root_left.shape[1]
    total = len(pieces)
    layout = (slots, halves, CHUNKS, total // CHUNKS, rows, cols)
    grad, *outs = pl.pallas_call(
        functools.partial(precondition_kernel, total),
        out_shape=[jax.ShapeDtypeStruct(layout, dtype)] + [jax.ShapeDtypeStruct(pieces[0].shape, dtype)] * total,
        in_specs=[SMEM, SMEM] + [ANY] * total + [HBM] * 2,
        out_specs=[ANY] * (total + 1),
        scratch_shapes=[
            pltpu.VMEM(layout, dtype),
            pltpu.VMEM(root_left.shape, dtype),
            pltpu.VMEM(root_right.shape, dtype),
            pltpu.VMEM(layout, dtype),
            pltpu.SemaphoreType.DMA((total,)),
            pltpu.SemaphoreType.DMA((2, slots)),
            pltpu.SemaphoreType.DMA((slots,)),
            pltpu.SemaphoreType.DMA((slots, total)),
        ],
        compiler_params=vmem(16),
        cost_estimate=cost(10 * slots * block * block, 4 * slots * block**3),
        name="precondition",
    )(used, me, *pieces, root_left, root_right)
    return grad.reshape(slots, block, block), outs[: total // CHUNKS], outs[total // CHUNKS :]


def unpack_kernel(index_ref, pieces_ref, out_ref, stage, in_sems, out_sem):
    cols = pieces_ref.shape[2]
    run_all(
        [
            pltpu.make_async_copy(pieces_ref.at[index_ref[w]], stage.at[:, pl.ds(w * cols, cols)], in_sems.at[w])
            for w in range(index_ref.shape[0])
        ]
    )
    run_all([pltpu.make_async_copy(stage, out_ref, out_sem)])


def unpack(index, pieces):
    _, rows, cols = pieces.shape
    shape = (rows, index.shape[0] * cols)
    return pl.pallas_call(
        unpack_kernel,
        out_shape=jax.ShapeDtypeStruct(shape, pieces.dtype),
        in_specs=[SMEM, ANY],
        out_specs=ANY,
        scratch_shapes=[
            pltpu.VMEM(shape, pieces.dtype),
            pltpu.SemaphoreType.DMA((index.shape[0],)),
            pltpu.SemaphoreType.DMA,
        ],
        cost_estimate=cost(4 * rows * shape[1]),
        compiler_params=vmem(4),
        name="unpack",
    )(index, pieces)


def place_kernel(base, quarter, places, me_ref, *refs):
    parts = refs[: len(places)]
    out_ref, stage, in_sems, out_sems = refs[-4:]
    me = me_ref[0]
    loads, stores = [], []
    filled = 0
    for i, (offset, down) in enumerate(places):
        rows = parts[i].shape[0]
        held = stage.at[pl.ds(filled, rows)]
        filled += rows
        start = pl.multiple_of(base + (me + offset) % 4 * quarter + down, quarter // 2)
        loads.append(pltpu.make_async_copy(parts[i], held, in_sems.at[i]))
        stores.append(pltpu.make_async_copy(held, out_ref.at[pl.ds(start, rows)], out_sems.at[i]))
    for load in loads:
        load.start()
    for load, store in zip(loads, stores):
        load.wait()
        store.start()
    for store in stores:
        store.wait()


def spread(own):
    return shift(own, -1), shift(own, 1)


def spread_far(from_next, from_prev):
    half = from_prev.shape[0] // 2
    return shift(from_prev[:half], 1), shift(from_next[half:], -1)


def place(me, near, far, updates, base, quarter, total_rows):
    places = ((0, 0), (1, 0), (3, 0)) * (len(near) > 0) + ((2, 0), (2, quarter // 2)) * (len(far) > 0)
    parts = [*near, *far]
    rows = sum(part.shape[0] for part in parts)
    width = parts[0].shape[1]
    operands = [me, *parts]
    aliases = {}
    if updates is not None:
        aliases = {len(operands): 0}
        operands.append(updates)
    return pl.pallas_call(
        functools.partial(place_kernel, base, quarter, places),
        out_shape=jax.ShapeDtypeStruct((total_rows, width), parts[0].dtype),
        in_specs=[SMEM] + [ANY] * len(parts) + [HBM] * len(aliases),
        out_specs=HBM,
        scratch_shapes=[
            pltpu.VMEM((rows, width), parts[0].dtype),
            pltpu.SemaphoreType.DMA((len(parts),)),
            pltpu.SemaphoreType.DMA((len(parts),)),
        ],
        input_output_aliases=aliases,
        cost_estimate=cost(4 * rows * width),
        compiler_params=vmem(4),
        name="place",
    )(*operands)


def expert_exchange(x):
    return lax.all_to_all(x, "expert", split_axis=0, concat_axis=0, tiled=True)


def replica_exchange(parts):
    return [parts[0]] + [shift(parts[d], d) for d in range(1, len(parts))]


def shards(grad_parts, owner_slot, stat_left, stat_right, root_left, root_right):
    dp_count = lax.axis_size("dp")
    expert_count = lax.axis_size("expert")
    shard_rows = grad_parts.shape[1]
    row_width = grad_parts.shape[2]
    slot_count, block_rows, block_cols = stat_left.shape
    wide_count = row_width // block_cols
    halves = block_rows // shard_rows
    row_blocks = expert_count // halves
    block_count = owner_slot.shape[0]
    chunk_rows = shard_rows // CHUNKS
    quarter = chunk_rows // dp_count
    half = quarter // 2
    held_count = dp_count * slot_count

    my_expert = lax.axis_index("expert")
    my_dp = lax.axis_index("dp")
    me = my_dp.astype(jnp.int32).reshape(1)
    blocks = jnp.arange(block_count, dtype=jnp.int32)
    column = owner_slot // slot_count % expert_count

    my_column = lax.dynamic_slice(column, (my_expert // halves * wide_count,), (wide_count,))
    to_column = my_column[None, :] == jnp.arange(expert_count, dtype=jnp.int32)[:, None]
    pieces = jnp.arange(wide_count, dtype=jnp.int32)
    send_piece = jnp.sum(jnp.where(to_column, pieces[None, :], 0), axis=1)

    held = jnp.arange(held_count, dtype=jnp.int32)

    def held_rows(replica):
        slot_ids = (replica * expert_count + my_expert) * slot_count + held % slot_count
        holds = owner_slot[None, :] == slot_ids[:, None]
        return jnp.sum(jnp.where(holds, blocks[None, :] // wide_count, 0), axis=1), jnp.sum(holds.astype(jnp.int32), axis=1)

    ahead = held // slot_count
    rows_ahead = held_rows((my_dp + ahead) % dp_count)
    rows_behind = held_rows((my_dp + dp_count - ahead) % dp_count)
    my_used = rows_ahead[1][:slot_count]

    def part(chunk, offset, down, rows):
        start = chunk * chunk_rows + (my_dp + offset) % dp_count * quarter + down
        return lax.dynamic_slice(grad_parts, (0, start, 0), (1, rows, row_width))[0]

    def toward(chunk, from_next, from_prev):
        to_prev = add(part(chunk, 3, 0, quarter), jnp.pad(from_next, ((0, half), (0, 0))))
        to_next = add(part(chunk, 1, 0, quarter), jnp.pad(from_prev, ((half, 0), (0, 0))))
        return to_prev, to_next

    def packed(chunk, to_prev, to_next):
        return pack(send_piece, part(chunk, 0, 0, quarter), shift(to_prev, -1), shift(to_next, 1), block_cols)

    entry = (row_blocks, halves, quarter, block_cols)

    def to_owners(incoming):
        return replica_exchange(to_slots(*rows_ahead, incoming.reshape(entry), dp_count))

    def to_rows(column_parts):
        return from_slots(*rows_behind, column_parts, row_blocks).reshape(expert_count, quarter, block_cols)

    from_next = shift(jnp.concatenate([part(chunk, 2, 0, half) for chunk in range(CHUNKS)]), -1)
    from_prev = shift(jnp.concatenate([part(chunk, 2, half, half) for chunk in range(CHUNKS)]), 1)
    first_packed = packed(0, *toward(0, from_next[:half], from_prev[:half]))
    sends = toward(1, from_next[half:], from_prev[half:])
    sends, first_packed = lax.optimization_barrier((sends, first_packed))
    first_in = expert_exchange(first_packed)
    second_in = expert_exchange(packed(1, *sends))
    first_owned = to_owners(first_in)
    first_owned, second_in = lax.optimization_barrier((first_owned, second_in))
    second_owned = to_owners(second_in)

    grad, first_out, second_out = precondition(my_used, me, first_owned + second_owned, root_left, root_right)

    first_back = replica_exchange(first_out)
    left_gram = jnp.einsum("sij,skj->sik", grad, grad, preferred_element_type=jnp.float32)
    right_gram = jnp.einsum("sji,sjk->sik", grad, grad, preferred_element_type=jnp.float32)
    new_left = DECAY_RATE * stat_left + (1.0 - DECAY_RATE) * left_gram
    new_right = DECAY_RATE * stat_right + (1.0 - DECAY_RATE) * right_gram
    first_back, new_left, new_right = lax.optimization_barrier((first_back, new_left, new_right))
    first_rows = to_rows(first_back)
    second_out, first_rows = lax.optimization_barrier((second_out, first_rows))
    first_in, second_rows = lax.optimization_barrier(
        (expert_exchange(first_rows), to_rows(replica_exchange(second_out)))
    )
    first_own, second_rows = lax.optimization_barrier((unpack(my_column, first_in), second_rows))
    second_in = expert_exchange(second_rows)

    near = spread(first_own)
    far = spread_far(*near)
    far, second_in = lax.optimization_barrier((far, second_in))
    second_own = unpack(my_column, second_in)
    updates = place(me, (first_own, *near), far, None, 0, quarter, shard_rows)
    near = spread(second_own)
    near, updates = lax.optimization_barrier((near, updates))
    far = spread_far(*near)
    updates = place(me, (second_own, *near), (), updates, chunk_rows, quarter, shard_rows)
    far, updates = lax.optimization_barrier((far, updates))
    updates = place(me, (), far, updates, chunk_rows, quarter, shard_rows)
    return new_left, new_right, updates


def solution(mesh):
    owned = P(("dp", "expert"), None, None)
    return jax.shard_map(
        shards,
        mesh=mesh,
        in_specs=(P("dp", "expert", None), P(), owned, owned, owned, owned),
        out_specs=(owned, owned, P("expert", None)),
        check_vma=False,
    )
```

```python
import functools

import jax
import jax.numpy as jnp
from jax import lax
from jax.experimental import pallas as pl
from jax.experimental.pallas import tpu as pltpu
from jax.sharding import PartitionSpec as P

DECAY_RATE = 0.999
CHUNKS = 2
ANY = pl.BlockSpec(memory_space=pl.ANY)
SMEM = pl.BlockSpec(memory_space=pltpu.SMEM)
HBM = pl.BlockSpec(memory_space=pltpu.HBM)


def shift(x, step):
    count = lax.axis_size("dp")
    return lax.ppermute(x, "dp", [(i, (i + step) % count) for i in range(count)])


def add(*terms):
    total = terms[0].astype(jnp.float32)
    for term in terms[1:]:
        total += term.astype(jnp.float32)
    return total.astype(terms[0].dtype)


def run_all(copies):
    for copy in copies:
        copy.start()
    for copy in copies:
        copy.wait()


def cost(moved, flops=0):
    return pl.CostEstimate(flops=flops, bytes_accessed=moved, transcendentals=0)


def vmem(mebibytes):
    return pltpu.CompilerParams(vmem_limit_bytes=mebibytes * 1024 * 1024)


def pack_kernel(index_ref, *refs):
    terms, (out_ref, held, pieces, in_sems, out_sems) = refs[:-5], refs[-5:]
    wide_count, _, block_cols = pieces.shape
    run_all([pltpu.make_async_copy(term, held.at[i], in_sems.at[i]) for i, term in enumerate(terms)])
    for w in range(wide_count):
        cols = slice(w * block_cols, (w + 1) * block_cols)
        pieces[w] = add(*(held[i, :, cols] for i in range(len(terms))))
    run_all(
        [
            pltpu.make_async_copy(pieces.at[index_ref[c]], out_ref.at[c], out_sems.at[c])
            for c in range(out_ref.shape[0])
        ]
    )


def pack(index, terms, block_cols):
    rows, width = terms[0].shape
    dtype = terms[0].dtype
    dests = index.shape[0]
    count = len(terms)
    return pl.pallas_call(
        pack_kernel,
        out_shape=jax.ShapeDtypeStruct((dests, rows, block_cols), dtype),
        in_specs=[SMEM] + [ANY] * count,
        out_specs=ANY,
        scratch_shapes=[
            pltpu.VMEM((count, rows, width), dtype),
            pltpu.VMEM((width // block_cols, rows, block_cols), dtype),
            pltpu.SemaphoreType.DMA((count,)),
            pltpu.SemaphoreType.DMA((dests,)),
        ],
        cost_estimate=cost(2 * (count + 1) * rows * width + 2 * dests * rows * block_cols),
        compiler_params=vmem(5),
        name="pack",
    )(index, *terms)


def stage_kernel(left_ref, right_ref, left_out, right_out, left, right, sems):
    run_all([pltpu.make_async_copy(left_ref, left, sems.at[0]), pltpu.make_async_copy(right_ref, right, sems.at[1])])
    run_all([pltpu.make_async_copy(left, left_out, sems.at[2]), pltpu.make_async_copy(right, right_out, sems.at[3])])


def stage(left, right):
    return pl.pallas_call(
        stage_kernel,
        out_shape=[jax.ShapeDtypeStruct(x.shape, x.dtype) for x in (left, right)],
        in_specs=[HBM, HBM],
        out_specs=[ANY, ANY],
        scratch_shapes=[
            pltpu.VMEM(left.shape, left.dtype),
            pltpu.VMEM(right.shape, right.dtype),
            pltpu.SemaphoreType.DMA((4,)),
        ],
        cost_estimate=cost(8 * left.size),
        compiler_params=vmem(5),
        name="stage",
    )(left, right)


def run_used(used_ref, copies):
    for start in (True, False):
        for i, copy in enumerate(copies):

            @pl.when(used_ref[i] > 0)
            def _():
                copy.start() if start else copy.wait()


def to_slots_kernel(row_ref, used_ref, rows_ref, *refs):
    outs, sems = refs[:-1], refs[-1]
    slots = outs[0].shape[0]
    run_used(
        used_ref,
        [
            pltpu.make_async_copy(rows_ref.at[row_ref[i]], outs[i // slots].at[i % slots], sems.at[i])
            for i in range(len(outs) * slots)
        ],
    )


def to_slots(row, used, rows, replicas):
    entry = rows.shape[1:]
    held = row.shape[0]
    return pl.pallas_call(
        to_slots_kernel,
        out_shape=[jax.ShapeDtypeStruct((held // replicas, *entry), rows.dtype)] * replicas,
        in_specs=[SMEM, SMEM, ANY],
        out_specs=[ANY] * replicas,
        scratch_shapes=[pltpu.SemaphoreType.DMA((held,))],
        cost_estimate=cost(4 * held * entry[0] * entry[1] * entry[2]),
        compiler_params=vmem(4),
        name="to_slots",
    )(row, used, rows)


def from_slots_kernel(row_ref, used_ref, *refs):
    parts, rows_ref, sems = refs[:-2], refs[-2], refs[-1]
    slots = parts[0].shape[0]
    run_used(
        used_ref,
        [
            pltpu.make_async_copy(parts[i // slots].at[i % slots], rows_ref.at[row_ref[i]], sems.at[i])
            for i in range(len(parts) * slots)
        ],
    )


def from_slots(row, used, parts, row_blocks):
    slots, *entry = parts[0].shape
    held = row.shape[0]
    return pl.pallas_call(
        from_slots_kernel,
        out_shape=jax.ShapeDtypeStruct((row_blocks, *entry), parts[0].dtype),
        in_specs=[SMEM, SMEM] + [ANY] * len(parts),
        out_specs=ANY,
        scratch_shapes=[pltpu.SemaphoreType.DMA((held,))],
        cost_estimate=cost(4 * held * entry[0] * entry[1] * entry[2]),
        compiler_params=vmem(4),
        name="from_slots",
    )(row, used, *parts)


def precondition_kernel(chunk_pieces, used_ref, me_ref, *refs):
    pieces, (left_ref, right_ref, grad_ref) = refs[:chunk_pieces], refs[chunk_pieces : chunk_pieces + 3]
    outs = refs[chunk_pieces + 3 : 2 * chunk_pieces + 3]
    grad, left, right, update, in_sems, root_sems, grad_sems, out_sems = refs[2 * chunk_pieces + 3 :]
    slots, _, _, count = grad.shape[:4]
    block = left.shape[1]
    me = me_ref[0]
    loads = [
        pltpu.make_async_copy(piece, grad.at[:, :, i // count, (me + count - i % count) % count], in_sems.at[i])
        for i, piece in enumerate(pieces)
    ]
    roots = [
        (
            pltpu.make_async_copy(left_ref.at[s], left.at[s], root_sems.at[0, s]),
            pltpu.make_async_copy(right_ref.at[s], right.at[s], root_sems.at[1, s]),
        )
        for s in range(slots)
    ]
    for pair in roots:
        for copy in pair:
            copy.start()
    run_all(loads)
    stores = []
    for s in range(slots):
        whole = grad[s].reshape(block, block)
        whole = jnp.where(used_ref[s] > 0, whole, jnp.zeros_like(whole))
        grad[s] = whole.reshape(grad.shape[1:])
        roots[s][0].wait()
        part = jnp.dot(left[s], whole, preferred_element_type=jnp.float32).astype(whole.dtype)
        roots[s][1].wait()
        result = jnp.dot(part, right[s], preferred_element_type=jnp.float32).astype(whole.dtype)
        update[s] = result.reshape(update.shape[1:])
        sends = [pltpu.make_async_copy(grad.at[s], grad_ref.at[s], grad_sems.at[s])] + [
            pltpu.make_async_copy(update.at[s, :, i // count, (me + i % count) % count], out.at[s], out_sems.at[s, i])
            for i, out in enumerate(outs)
        ]
        for copy in sends:
            copy.start()
        stores += sends
    for copy in stores:
        copy.wait()


def precondition(used, me, pieces, root_left, root_right):
    slots, halves, rows, cols = pieces[0].shape
    dtype = pieces[0].dtype
    block = root_left.shape[1]
    total = len(pieces)
    layout = (slots, halves, CHUNKS, total // CHUNKS, rows, cols)
    grad, *outs = pl.pallas_call(
        functools.partial(precondition_kernel, total),
        out_shape=[jax.ShapeDtypeStruct(layout, dtype)] + [jax.ShapeDtypeStruct(pieces[0].shape, dtype)] * total,
        in_specs=[SMEM, SMEM] + [ANY] * (total + 2),
        out_specs=[ANY] * (total + 1),
        scratch_shapes=[
            pltpu.VMEM(layout, dtype),
            pltpu.VMEM(root_left.shape, dtype),
            pltpu.VMEM(root_right.shape, dtype),
            pltpu.VMEM(layout, dtype),
            pltpu.SemaphoreType.DMA((total,)),
            pltpu.SemaphoreType.DMA((2, slots)),
            pltpu.SemaphoreType.DMA((slots,)),
            pltpu.SemaphoreType.DMA((slots, total)),
        ],
        compiler_params=vmem(16),
        cost_estimate=cost(10 * slots * block * block, 4 * slots * block**3),
        name="precondition",
    )(used, me, *pieces, root_left, root_right)
    return grad.reshape(slots, block, block), outs[: total // CHUNKS], outs[total // CHUNKS :]


def unpack_kernel(index_ref, pieces_ref, out_ref, stage, in_sems, out_sem):
    cols = pieces_ref.shape[2]
    run_all(
        [
            pltpu.make_async_copy(pieces_ref.at[index_ref[w]], stage.at[:, pl.ds(w * cols, cols)], in_sems.at[w])
            for w in range(index_ref.shape[0])
        ]
    )
    run_all([pltpu.make_async_copy(stage, out_ref, out_sem)])


def unpack(index, pieces):
    _, rows, cols = pieces.shape
    shape = (rows, index.shape[0] * cols)
    return pl.pallas_call(
        unpack_kernel,
        out_shape=jax.ShapeDtypeStruct(shape, pieces.dtype),
        in_specs=[SMEM, ANY],
        out_specs=ANY,
        scratch_shapes=[
            pltpu.VMEM(shape, pieces.dtype),
            pltpu.SemaphoreType.DMA((index.shape[0],)),
            pltpu.SemaphoreType.DMA,
        ],
        cost_estimate=cost(4 * rows * shape[1]),
        compiler_params=vmem(4),
        name="unpack",
    )(index, pieces)


def place_kernel(base, quarter, places, me_ref, *refs):
    parts = refs[: len(places)]
    out_ref, stage, in_sems, out_sems = refs[-4:]
    me = me_ref[0]
    loads, stores = [], []
    filled = 0
    for i, (offset, down) in enumerate(places):
        rows = parts[i].shape[0]
        held = stage.at[pl.ds(filled, rows)]
        filled += rows
        start = pl.multiple_of(base + (me + offset) % 4 * quarter + down, quarter // 2)
        loads.append(pltpu.make_async_copy(parts[i], held, in_sems.at[i]))
        stores.append(pltpu.make_async_copy(held, out_ref.at[pl.ds(start, rows)], out_sems.at[i]))
    for load in loads:
        load.start()
    for load, store in zip(loads, stores):
        load.wait()
        store.start()
    for store in stores:
        store.wait()


def spread(own):
    return shift(own, -1), shift(own, 1)


def spread_far(from_next, from_prev):
    half = from_prev.shape[0] // 2
    return shift(from_prev[:half], 1), shift(from_next[half:], -1)


def place(me, near, far, updates, base, quarter, total_rows):
    places = ((0, 0), (1, 0), (3, 0)) * (len(near) > 0) + ((2, 0), (2, quarter // 2)) * (len(far) > 0)
    parts = [*near, *far]
    rows = sum(part.shape[0] for part in parts)
    width = parts[0].shape[1]
    operands = [me, *parts]
    aliases = {}
    if updates is not None:
        aliases = {len(operands): 0}
        operands.append(updates)
    return pl.pallas_call(
        functools.partial(place_kernel, base, quarter, places),
        out_shape=jax.ShapeDtypeStruct((total_rows, width), parts[0].dtype),
        in_specs=[SMEM] + [ANY] * len(parts) + [HBM] * len(aliases),
        out_specs=HBM,
        scratch_shapes=[
            pltpu.VMEM((rows, width), parts[0].dtype),
            pltpu.SemaphoreType.DMA((len(parts),)),
            pltpu.SemaphoreType.DMA((len(parts),)),
        ],
        input_output_aliases=aliases,
        cost_estimate=cost(4 * rows * width),
        compiler_params=vmem(4),
        name="place",
    )(*operands)


def expert_exchange(x):
    return lax.all_to_all(x, "expert", split_axis=0, concat_axis=0, tiled=True)


def replica_exchange(parts):
    return [parts[0]] + [shift(parts[d], d) for d in range(1, len(parts))]


def shards(grad_parts, owner_slot, stat_left, stat_right, root_left, root_right):
    dp_count = lax.axis_size("dp")
    expert_count = lax.axis_size("expert")
    shard_rows = grad_parts.shape[1]
    row_width = grad_parts.shape[2]
    slot_count, block_rows, block_cols = stat_left.shape
    wide_count = row_width // block_cols
    halves = block_rows // shard_rows
    row_blocks = expert_count // halves
    block_count = owner_slot.shape[0]
    chunk_rows = shard_rows // CHUNKS
    quarter = chunk_rows // dp_count
    held_count = dp_count * slot_count

    my_expert = lax.axis_index("expert")
    my_dp = lax.axis_index("dp")
    me = my_dp.astype(jnp.int32).reshape(1)
    blocks = jnp.arange(block_count, dtype=jnp.int32)
    column = owner_slot // slot_count % expert_count

    my_column = lax.dynamic_slice(column, (my_expert // halves * wide_count,), (wide_count,))
    to_column = my_column[None, :] == jnp.arange(expert_count, dtype=jnp.int32)[:, None]
    pieces = jnp.arange(wide_count, dtype=jnp.int32)
    send_piece = jnp.sum(jnp.where(to_column, pieces[None, :], 0), axis=1)

    held = jnp.arange(held_count, dtype=jnp.int32)

    def held_rows(replica):
        slot_ids = (replica * expert_count + my_expert) * slot_count + held % slot_count
        holds = owner_slot[None, :] == slot_ids[:, None]
        return jnp.sum(jnp.where(holds, blocks[None, :] // wide_count, 0), axis=1), jnp.sum(holds.astype(jnp.int32), axis=1)

    ahead = held // slot_count
    rows_ahead = held_rows((my_dp + ahead) % dp_count)
    rows_behind = held_rows((my_dp + dp_count - ahead) % dp_count)
    my_used = rows_ahead[1][:slot_count]

    def part(chunk, offset, down, rows):
        start = chunk * chunk_rows + (my_dp + offset) % dp_count * quarter + down
        return lax.dynamic_slice(grad_parts, (0, start, 0), (1, rows, row_width))[0]

    def parts(chunk):
        return [part(chunk, offset, 0, quarter) for offset in range(dp_count)]

    entry = (row_blocks, halves, quarter, block_cols)

    def to_owners(incoming):
        return replica_exchange(to_slots(*rows_ahead, incoming.reshape(entry), dp_count))

    def to_rows(column_parts):
        return from_slots(*rows_behind, column_parts, row_blocks).reshape(expert_count, quarter, block_cols)

    first_terms = replica_exchange(parts(0))
    second_parts, first_terms = lax.optimization_barrier((parts(1), first_terms))
    second_terms = replica_exchange(second_parts)
    first_in = expert_exchange(pack(send_piece, first_terms, block_cols))
    second_in = expert_exchange(pack(send_piece, second_terms, block_cols))
    first_owned = to_owners(first_in)
    first_owned, second_in, (left, right) = lax.optimization_barrier(
        (first_owned, second_in, stage(root_left, root_right))
    )
    second_owned = to_owners(second_in)

    grad, first_out, second_out = precondition(my_used, me, first_owned + second_owned, left, right)

    first_back = replica_exchange(first_out)
    left_gram = jnp.einsum("sij,skj->sik", grad, grad, preferred_element_type=jnp.float32)
    right_gram = jnp.einsum("sji,sjk->sik", grad, grad, preferred_element_type=jnp.float32)
    new_left = DECAY_RATE * stat_left + (1.0 - DECAY_RATE) * left_gram
    new_right = DECAY_RATE * stat_right + (1.0 - DECAY_RATE) * right_gram
    first_back, new_left, new_right = lax.optimization_barrier((first_back, new_left, new_right))
    first_rows = to_rows(first_back)
    second_out, first_rows = lax.optimization_barrier((second_out, first_rows))
    first_in, second_rows = lax.optimization_barrier(
        (expert_exchange(first_rows), to_rows(replica_exchange(second_out)))
    )
    first_own, second_rows = lax.optimization_barrier((unpack(my_column, first_in), second_rows))
    second_in = expert_exchange(second_rows)

    near, second_in = lax.optimization_barrier((spread(first_own), second_in))
    far = spread_far(*near)
    second_own = unpack(my_column, second_in)
    updates = place(me, (first_own, *near), far, None, 0, quarter, shard_rows)
    near = spread(second_own)
    near, updates = lax.optimization_barrier((near, updates))
    far = spread_far(*near)
    updates = place(me, (second_own, *near), (), updates, chunk_rows, quarter, shard_rows)
    far, updates = lax.optimization_barrier((far, updates))
    updates = place(me, (), far, updates, chunk_rows, quarter, shard_rows)
    return new_left, new_right, updates


def solution(mesh):
    owned = P(("dp", "expert"), None, None)
    return jax.shard_map(
        shards,
        mesh=mesh,
        in_specs=(P("dp", "expert", None), P(), owned, owned, owned, owned),
        out_specs=(owned, owned, P("expert", None)),
        check_vma=False,
    )
```

```python
import functools

import jax
import jax.numpy as jnp
from jax import lax
from jax.experimental import pallas as pl
from jax.experimental.pallas import tpu as pltpu
from jax.sharding import PartitionSpec as P

DECAY_RATE = 0.999
CHUNKS = 2
ANY = pl.BlockSpec(memory_space=pl.ANY)
SMEM = pl.BlockSpec(memory_space=pltpu.SMEM)
HBM = pl.BlockSpec(memory_space=pltpu.HBM)
VMEM = pl.BlockSpec(memory_space=pltpu.VMEM)


def shift(x, step):
    count = lax.axis_size("dp")
    return lax.ppermute(x, "dp", [(i, (i + step) % count) for i in range(count)])


def add(*terms):
    total = terms[0].astype(jnp.float32)
    for term in terms[1:]:
        total += term.astype(jnp.float32)
    return total.astype(terms[0].dtype)


def run_all(copies):
    for copy in copies:
        copy.start()
    for copy in copies:
        copy.wait()


def cost(moved, flops=0):
    return pl.CostEstimate(flops=flops, bytes_accessed=moved, transcendentals=0)


def vmem(mebibytes):
    return pltpu.CompilerParams(vmem_limit_bytes=mebibytes * 1024 * 1024)


def pack_kernel(index_ref, own_ref, next_ref, prev_ref, out_ref, own, near, far, pieces, in_sems, out_sems):
    wide_count, _, block_cols = pieces.shape
    run_all(
        [
            pltpu.make_async_copy(own_ref, own, in_sems.at[0]),
            pltpu.make_async_copy(next_ref, near, in_sems.at[1]),
            pltpu.make_async_copy(prev_ref, far, in_sems.at[2]),
        ]
    )
    for w in range(wide_count):
        cols = slice(w * block_cols, (w + 1) * block_cols)
        pieces[w] = add(own[:, cols], near[:, cols], far[:, cols])
    run_all(
        [
            pltpu.make_async_copy(pieces.at[index_ref[c]], out_ref.at[c], out_sems.at[c])
            for c in range(out_ref.shape[0])
        ]
    )


def pack(index, own, from_next, from_prev, block_cols):
    rows, width = own.shape
    dests = index.shape[0]
    return pl.pallas_call(
        pack_kernel,
        out_shape=jax.ShapeDtypeStruct((dests, rows, block_cols), own.dtype),
        in_specs=[SMEM, ANY, ANY, ANY],
        out_specs=ANY,
        scratch_shapes=[pltpu.VMEM((rows, width), own.dtype)] * 3
        + [
            pltpu.VMEM((width // block_cols, rows, block_cols), own.dtype),
            pltpu.SemaphoreType.DMA((3,)),
            pltpu.SemaphoreType.DMA((dests,)),
        ],
        cost_estimate=cost(8 * rows * width + 2 * dests * rows * block_cols),
        compiler_params=vmem(4),
        name="pack",
    )(index, own, from_next, from_prev)


def run_used(used_ref, copies):
    for start in (True, False):
        for i, copy in enumerate(copies):

            @pl.when(used_ref[i] > 0)
            def _():
                copy.start() if start else copy.wait()


def to_slots_kernel(row_ref, used_ref, rows_ref, *refs):
    outs, sems = refs[:-1], refs[-1]
    slots = outs[0].shape[0]
    run_used(
        used_ref,
        [
            pltpu.make_async_copy(rows_ref.at[row_ref[i]], outs[i // slots].at[i % slots], sems.at[i])
            for i in range(len(outs) * slots)
        ],
    )


def to_slots(row, used, rows, replicas):
    entry = rows.shape[1:]
    held = row.shape[0]
    return pl.pallas_call(
        to_slots_kernel,
        out_shape=[jax.ShapeDtypeStruct((held // replicas, *entry), rows.dtype)] * replicas,
        in_specs=[SMEM, SMEM, ANY],
        out_specs=[ANY] * replicas,
        scratch_shapes=[pltpu.SemaphoreType.DMA((held,))],
        cost_estimate=cost(4 * held * entry[0] * entry[1] * entry[2]),
        compiler_params=vmem(4),
        name="to_slots",
    )(row, used, rows)


def from_slots_kernel(row_ref, used_ref, *refs):
    parts, rows_ref, sems = refs[:-2], refs[-2], refs[-1]
    slots = parts[0].shape[0]
    run_used(
        used_ref,
        [
            pltpu.make_async_copy(parts[i // slots].at[i % slots], rows_ref.at[row_ref[i]], sems.at[i])
            for i in range(len(parts) * slots)
        ],
    )


def from_slots(row, used, parts, row_blocks):
    slots, *entry = parts[0].shape
    held = row.shape[0]
    return pl.pallas_call(
        from_slots_kernel,
        out_shape=jax.ShapeDtypeStruct((row_blocks, *entry), parts[0].dtype),
        in_specs=[SMEM, SMEM] + [ANY] * len(parts),
        out_specs=ANY,
        scratch_shapes=[pltpu.SemaphoreType.DMA((held,))],
        cost_estimate=cost(4 * held * entry[0] * entry[1] * entry[2]),
        compiler_params=vmem(4),
        name="from_slots",
    )(row, used, *parts)


def precondition_kernel(chunk_pieces, used_ref, me_ref, *refs):
    pieces, (left, right, grad_ref) = refs[:chunk_pieces], refs[chunk_pieces : chunk_pieces + 3]
    outs = refs[chunk_pieces + 3 : 2 * chunk_pieces + 3]
    grad, update, in_sems, grad_sems, out_sems = refs[2 * chunk_pieces + 3 :]
    slots, _, _, count = grad.shape[:4]
    block = left.shape[1]
    me = me_ref[0]
    loads = [
        pltpu.make_async_copy(piece, grad.at[:, :, i // count, (me + count - i % count) % count], in_sems.at[i])
        for i, piece in enumerate(pieces)
    ]
    run_all(loads)
    stores = []
    for s in range(slots):
        whole = grad[s].reshape(block, block)
        whole = jnp.where(used_ref[s] > 0, whole, jnp.zeros_like(whole))
        grad[s] = whole.reshape(grad.shape[1:])
        part = jnp.dot(left[s], whole, preferred_element_type=jnp.float32).astype(whole.dtype)
        result = jnp.dot(part, right[s], preferred_element_type=jnp.float32).astype(whole.dtype)
        update[s] = result.reshape(update.shape[1:])
        sends = [pltpu.make_async_copy(grad.at[s], grad_ref.at[s], grad_sems.at[s])] + [
            pltpu.make_async_copy(update.at[s, :, i // count, (me + i % count) % count], out.at[s], out_sems.at[s, i])
            for i, out in enumerate(outs)
        ]
        for copy in sends:
            copy.start()
        stores += sends
    for copy in stores:
        copy.wait()


def precondition(used, me, pieces, root_left, root_right):
    slots, halves, rows, cols = pieces[0].shape
    dtype = pieces[0].dtype
    block = root_left.shape[1]
    total = len(pieces)
    layout = (slots, halves, CHUNKS, total // CHUNKS, rows, cols)
    grad, *outs = pl.pallas_call(
        functools.partial(precondition_kernel, total),
        out_shape=[jax.ShapeDtypeStruct(layout, dtype)] + [jax.ShapeDtypeStruct(pieces[0].shape, dtype)] * total,
        in_specs=[SMEM, SMEM] + [ANY] * total + [VMEM] * 2,
        out_specs=[ANY] * (total + 1),
        scratch_shapes=[
            pltpu.VMEM(layout, dtype),
            pltpu.VMEM(layout, dtype),
            pltpu.SemaphoreType.DMA((total,)),
            pltpu.SemaphoreType.DMA((slots,)),
            pltpu.SemaphoreType.DMA((slots, total)),
        ],
        compiler_params=vmem(16),
        cost_estimate=cost(10 * slots * block * block, 4 * slots * block**3),
        name="precondition",
    )(used, me, *pieces, root_left, root_right)
    return grad.reshape(slots, block, block), outs[: total // CHUNKS], outs[total // CHUNKS :]


def unpack_kernel(index_ref, pieces_ref, out_ref, stage, in_sems, out_sem):
    cols = pieces_ref.shape[2]
    run_all(
        [
            pltpu.make_async_copy(pieces_ref.at[index_ref[w]], stage.at[:, pl.ds(w * cols, cols)], in_sems.at[w])
            for w in range(index_ref.shape[0])
        ]
    )
    run_all([pltpu.make_async_copy(stage, out_ref, out_sem)])


def unpack(index, pieces):
    _, rows, cols = pieces.shape
    shape = (rows, index.shape[0] * cols)
    return pl.pallas_call(
        unpack_kernel,
        out_shape=jax.ShapeDtypeStruct(shape, pieces.dtype),
        in_specs=[SMEM, ANY],
        out_specs=ANY,
        scratch_shapes=[
            pltpu.VMEM(shape, pieces.dtype),
            pltpu.SemaphoreType.DMA((index.shape[0],)),
            pltpu.SemaphoreType.DMA,
        ],
        cost_estimate=cost(4 * rows * shape[1]),
        compiler_params=vmem(4),
        name="unpack",
    )(index, pieces)


def place_kernel(base, quarter, places, me_ref, *refs):
    parts = refs[: len(places)]
    out_ref, stage, in_sems, out_sems = refs[-4:]
    me = me_ref[0]
    loads, stores = [], []
    filled = 0
    for i, (offset, down) in enumerate(places):
        rows = parts[i].shape[0]
        held = stage.at[pl.ds(filled, rows)]
        filled += rows
        start = pl.multiple_of(base + (me + offset) % 4 * quarter + down, quarter // 2)
        loads.append(pltpu.make_async_copy(parts[i], held, in_sems.at[i]))
        stores.append(pltpu.make_async_copy(held, out_ref.at[pl.ds(start, rows)], out_sems.at[i]))
    for load in loads:
        load.start()
    for load, store in zip(loads, stores):
        load.wait()
        store.start()
    for store in stores:
        store.wait()


def spread(own):
    return shift(own, -1), shift(own, 1)


def spread_far(from_next, from_prev):
    half = from_prev.shape[0] // 2
    return shift(from_prev[:half], 1), shift(from_next[half:], -1)


def place(me, near, far, updates, base, quarter, total_rows):
    places = ((0, 0), (1, 0), (3, 0)) * (len(near) > 0) + ((2, 0), (2, quarter // 2)) * (len(far) > 0)
    parts = [*near, *far]
    rows = sum(part.shape[0] for part in parts)
    width = parts[0].shape[1]
    operands = [me, *parts]
    aliases = {}
    if updates is not None:
        aliases = {len(operands): 0}
        operands.append(updates)
    return pl.pallas_call(
        functools.partial(place_kernel, base, quarter, places),
        out_shape=jax.ShapeDtypeStruct((total_rows, width), parts[0].dtype),
        in_specs=[SMEM] + [ANY] * len(parts) + [HBM] * len(aliases),
        out_specs=HBM,
        scratch_shapes=[
            pltpu.VMEM((rows, width), parts[0].dtype),
            pltpu.SemaphoreType.DMA((len(parts),)),
            pltpu.SemaphoreType.DMA((len(parts),)),
        ],
        input_output_aliases=aliases,
        cost_estimate=cost(4 * rows * width),
        compiler_params=vmem(4),
        name="place",
    )(*operands)


def expert_exchange(x):
    return lax.all_to_all(x, "expert", split_axis=0, concat_axis=0, tiled=True)


def replica_exchange(parts):
    return [parts[0]] + [shift(parts[d], d) for d in range(1, len(parts))]


def shards(grad_parts, owner_slot, stat_left, stat_right, root_left, root_right):
    dp_count = lax.axis_size("dp")
    expert_count = lax.axis_size("expert")
    shard_rows = grad_parts.shape[1]
    row_width = grad_parts.shape[2]
    slot_count, block_rows, block_cols = stat_left.shape
    wide_count = row_width // block_cols
    halves = block_rows // shard_rows
    row_blocks = expert_count // halves
    block_count = owner_slot.shape[0]
    chunk_rows = shard_rows // CHUNKS
    quarter = chunk_rows // dp_count
    half = quarter // 2
    held_count = dp_count * slot_count

    my_expert = lax.axis_index("expert")
    my_dp = lax.axis_index("dp")
    me = my_dp.astype(jnp.int32).reshape(1)
    blocks = jnp.arange(block_count, dtype=jnp.int32)
    column = owner_slot // slot_count % expert_count

    my_column = lax.dynamic_slice(column, (my_expert // halves * wide_count,), (wide_count,))
    to_column = my_column[None, :] == jnp.arange(expert_count, dtype=jnp.int32)[:, None]
    pieces = jnp.arange(wide_count, dtype=jnp.int32)
    send_piece = jnp.sum(jnp.where(to_column, pieces[None, :], 0), axis=1)

    held = jnp.arange(held_count, dtype=jnp.int32)

    def held_rows(replica):
        slot_ids = (replica * expert_count + my_expert) * slot_count + held % slot_count
        holds = owner_slot[None, :] == slot_ids[:, None]
        return jnp.sum(jnp.where(holds, blocks[None, :] // wide_count, 0), axis=1), jnp.sum(holds.astype(jnp.int32), axis=1)

    ahead = held // slot_count
    rows_ahead = held_rows((my_dp + ahead) % dp_count)
    rows_behind = held_rows((my_dp + dp_count - ahead) % dp_count)
    my_used = rows_ahead[1][:slot_count]

    def part(chunk, offset, down, rows):
        start = chunk * chunk_rows + (my_dp + offset) % dp_count * quarter + down
        return lax.dynamic_slice(grad_parts, (0, start, 0), (1, rows, row_width))[0]

    def toward(chunk, from_next, from_prev):
        to_prev = add(part(chunk, 3, 0, quarter), jnp.pad(from_next, ((0, half), (0, 0))))
        to_next = add(part(chunk, 1, 0, quarter), jnp.pad(from_prev, ((half, 0), (0, 0))))
        return to_prev, to_next

    def packed(chunk, to_prev, to_next):
        return pack(send_piece, part(chunk, 0, 0, quarter), shift(to_prev, -1), shift(to_next, 1), block_cols)

    entry = (row_blocks, halves, quarter, block_cols)

    def to_owners(incoming):
        return replica_exchange(to_slots(*rows_ahead, incoming.reshape(entry), dp_count))

    def to_rows(column_parts):
        return from_slots(*rows_behind, column_parts, row_blocks).reshape(expert_count, quarter, block_cols)

    from_next = shift(jnp.concatenate([part(chunk, 2, 0, half) for chunk in range(CHUNKS)]), -1)
    from_prev = shift(jnp.concatenate([part(chunk, 2, half, half) for chunk in range(CHUNKS)]), 1)
    first_packed = packed(0, *toward(0, from_next[:half], from_prev[:half]))
    sends = toward(1, from_next[half:], from_prev[half:])
    sends, first_packed = lax.optimization_barrier((sends, first_packed))
    first_in = expert_exchange(first_packed)
    second_in = expert_exchange(packed(1, *sends))
    first_owned = to_owners(first_in)
    first_owned, second_in = lax.optimization_barrier((first_owned, second_in))
    second_owned = to_owners(second_in)

    grad, first_out, second_out = precondition(my_used, me, first_owned + second_owned, root_left, root_right)

    first_back = replica_exchange(first_out)
    left_gram = jnp.einsum("sij,skj->sik", grad, grad, preferred_element_type=jnp.float32)
    right_gram = jnp.einsum("sji,sjk->sik", grad, grad, preferred_element_type=jnp.float32)
    new_left = DECAY_RATE * stat_left + (1.0 - DECAY_RATE) * left_gram
    new_right = DECAY_RATE * stat_right + (1.0 - DECAY_RATE) * right_gram
    first_back, new_left, new_right = lax.optimization_barrier((first_back, new_left, new_right))
    first_rows = to_rows(first_back)
    second_out, first_rows = lax.optimization_barrier((second_out, first_rows))
    first_in, second_rows = lax.optimization_barrier(
        (expert_exchange(first_rows), to_rows(replica_exchange(second_out)))
    )
    first_own, second_rows = lax.optimization_barrier((unpack(my_column, first_in), second_rows))
    second_in = expert_exchange(second_rows)

    near = spread(first_own)
    far = spread_far(*near)
    far, second_own = lax.optimization_barrier((far, unpack(my_column, second_in)))
    updates = place(me, (first_own, *near), far, None, 0, quarter, shard_rows)
    near = spread(second_own)
    near, updates = lax.optimization_barrier((near, updates))
    far = spread_far(*near)
    updates = place(me, (second_own, *near), (), updates, chunk_rows, quarter, shard_rows)
    far, updates = lax.optimization_barrier((far, updates))
    updates = place(me, (), far, updates, chunk_rows, quarter, shard_rows)
    return new_left, new_right, updates


def solution(mesh):
    owned = P(("dp", "expert"), None, None)
    return jax.shard_map(
        shards,
        mesh=mesh,
        in_specs=(P("dp", "expert", None), P(), owned, owned, owned, owned),
        out_specs=(owned, owned, P("expert", None)),
        check_vma=False,
    )
```
